256 devices in a mesh: dp: 32 (over x, y, core), tensor: 8 (over z).
Axes of the slice: x: 4, y: 4, z: 8, core: 2. Of those that a mesh axis runs over, the one named last changes fastest.
Arguments:
- grad: bfloat16 [32, 8192, 1024], P('dp', None, 'tensor'), may hold values from -9 to 9
- error: float32 [32, 8192, 1024], P('dp', None, 'tensor'), may hold values from -4 to 4
- warm_q: float32 [1024, 64], P('tensor'), may hold values from -6 to 6
Outputs:
- update: bfloat16 [8192, 1024], P(None, 'tensor')
- new_error: float32 [32, 8192, 1024], P('dp', None, 'tensor')
- new_q: float32 [1024, 64], P('tensor')
The draws below stay inside these ranges and needn't reach their ends.
All inputs are finite; a program needn't handle non-finite values.
Results may differ from the reference program's by a relative error of at most 0.001.
Values sent between devices are 32-bit elements; how exact they have to be, the bound alone decides.
No kernel may reach another device: no remote copies, remote signals or barrier semaphores. Data moves between devices by JAX's collectives and lax.ppermute only.
A program may use at most 64 MiB of HBM per device.

```python
import jax
import jax.numpy as jnp
from jax import lax

D = 8192
KV = 1024
RANK = 64
REPLICAS = 32


def draw_grad(key, part):
    key = jax.random.fold_in(key, 11)
    key_left, key_right, key_noise = jax.random.split(key, 3)
    left = jax.random.truncated_normal(key_left, -3.0, 3.0, (D,), jnp.float32)
    right = jax.random.truncated_normal(key_right, -3.0, 3.0, (KV,), jnp.float32)
    common = 0.5 * left[:, None] * right[None, :]
    noise = jax.random.truncated_normal(key_noise, -3.0, 3.0, (REPLICAS, D, KV), jnp.float32)
    return (common[None, :, :] + noise).astype(jnp.bfloat16)


def levels(own_key, extent, pieces, low, high):
    def one(axis_at, blocks):
        steps = jax.random.uniform(jax.random.fold_in(jax.random.fold_in(own_key, 6), axis_at), (blocks,), jnp.float32, low / len(pieces), high / len(pieces))
        return jnp.repeat(jnp.exp(steps), extent[axis_at] // blocks).reshape((-1,) + (1,) * (len(extent) - axis_at - 1))

    factor_of = one(*pieces[0])
    for cut in pieces[1:]:
        factor_of = factor_of * one(*cut)
    return factor_of


def centred(key, extent, spread, reach, cuts=(), held_as=jnp.bfloat16):
    drawn = spread * jax.random.normal(key, extent, jnp.float32)
    if cuts:
        drawn = drawn * levels(key, extent, cuts, -0.22, 0.18)
    return jnp.clip(drawn, -reach, reach).astype(held_as)


def setup_inputs(seed: int = 0) -> dict:
    key_list = jax.random.split(jax.random.key(seed), 4)
    grad = draw_grad(jax.random.fold_in(key_list[3], 71), 0)
    error = centred(key_list[1], (REPLICAS, D, KV), 0.5, 4.0, ((0, 32), (2, 8)), jnp.float32)
    warm_q = centred(key_list[2], (KV, RANK), 1.0, 6.0, ((0, 8),), jnp.float32)
    return dict(grad=grad, error=error, warm_q=warm_q)


def reference(grad, error, warm_q):
    highest = lax.Precision.HIGHEST
    scale = 1.0 / REPLICAS

    def left_step(total, pair):
        combined = pair[0].astype(jnp.float32) + pair[1]
        return (total + jnp.dot(combined, warm_q, precision=highest), None)
    factor, _ = lax.scan(left_step, jnp.zeros((D, RANK), jnp.float32), (grad, error))
    factor = factor * scale
    gram = lax.dot_general(factor, factor, (((0,), (0,)), ((), ())), precision=highest)
    lower = jnp.linalg.cholesky(gram)
    basis = lax.linalg.triangular_solve(lower, factor, left_side=False, lower=True, transpose_a=True)

    def right_step(total, pair):
        combined = pair[0].astype(jnp.float32) + pair[1]
        return (total + lax.dot_general(combined, basis, (((0,), (0,)), ((), ())), precision=highest), None)
    new_q, _ = lax.scan(right_step, jnp.zeros((KV, RANK), jnp.float32), (grad, error))
    new_q = new_q * scale
    lowrank = lax.dot_general(basis, new_q, (((1,), (1,)), ((), ())), precision=highest)
    update = lowrank.astype(jnp.bfloat16)

    def residual_of(pair):
        return pair[0].astype(jnp.float32) + pair[1] - lowrank
    new_error = lax.map(residual_of, (grad, error))
    return (update, new_error, new_q)
```

```python
import jax
import jax.numpy as jnp
from jax import lax
from jax.experimental import pallas as pl
from jax.experimental.pallas import tpu as pltpu
from jax.sharding import Mesh, PartitionSpec as P

ROWS = 8192
COLS = 128
RANK = 64
HALF = ROWS // 4
BLOCK = 512
STEPS = HALF // BLOCK
REPLICAS = 32
PAIR_A = [(0, 1), (1, 0), (2, 3), (3, 2)]
PAIR_B = [(1, 2), (2, 1), (3, 0), (0, 3)]
VMEM_LIMIT = 48 * 1024 * 1024


def split2(a):
    high = a.astype(jnp.bfloat16)
    low = (a - high.astype(jnp.float32)).astype(jnp.bfloat16)
    return high, low


def mm(a, b):
    return jnp.dot(a, b, preferred_element_type=jnp.float32)


def mm_t(a, b):
    return lax.dot_general(a, b, (((0,), (0,)), ((), ())), preferred_element_type=jnp.float32)


def mm_highest(a, b, dims=((1,), (0,))):
    return lax.dot_general(a, b, (dims, ((), ())), precision=lax.Precision.HIGHEST, preferred_element_type=jnp.float32)


def left_kernel(half_ref, grad_ref, error_ref, warm_ref, term_ref, top_ref, bottom_ref):
    @pl.when(pl.program_id(0) == 0)
    def _():
        high, low = split2(warm_ref[...])
        none = jnp.zeros_like(high)
        top = jnp.concatenate([high, none, low, none], axis=1)
        bottom = jnp.concatenate([none, high, none, low], axis=1)
        top_ref[...] = jnp.concatenate([top, top], axis=0)
        bottom_ref[...] = jnp.concatenate([bottom, bottom], axis=0)

    combined = grad_ref[...].astype(jnp.float32) + error_ref[...]
    top = jnp.concatenate(split2(combined[0]), axis=1)
    bottom = jnp.concatenate(split2(combined[1]), axis=1)
    wide = mm(top, top_ref[...]) + mm(bottom, bottom_ref[...])
    term_ref[...] = wide[:, :128] + wide[:, 128:]


def left_half(half, grad, error, warm_q):
    rows = pl.BlockSpec((2, BLOCK, COLS), lambda i, half: (0, half[0] * STEPS + i, 0))
    return pl.pallas_call(
        left_kernel,
        out_shape=jax.ShapeDtypeStruct((HALF, 128), jnp.float32),
        grid_spec=pltpu.PrefetchScalarGridSpec(
            num_scalar_prefetch=1,
            grid=(STEPS,),
            in_specs=[rows, rows, pl.BlockSpec((COLS, RANK), lambda i, half: (0, 0))],
            out_specs=pl.BlockSpec((BLOCK, 128), lambda i, half: (i, 0)),
            scratch_shapes=[pltpu.VMEM((256, 256), jnp.bfloat16)] * 2,
        ),
        compiler_params=pltpu.CompilerParams(vmem_limit_bytes=VMEM_LIMIT),
        cost_estimate=pl.CostEstimate(flops=2 * 2 * HALF * 256 * 256, bytes_accessed=2 * HALF * COLS * 6 + HALF * 128 * 4, transcendentals=0),
        name="left",
    )(half, grad, error, warm_q)


def both_halves(i, half):
    own = half[0] * STEPS + i
    other = (1 - half[0]) * STEPS + i - STEPS
    return (0, jnp.where(i < STEPS, own, other), 0)


def right_kernel(half_ref, grad_ref, error_ref, own_ref, other_ref, right_ref, gram_ref, acc_ref, gram_acc_ref, tail_acc_ref):
    i = pl.program_id(0)

    @pl.when(i == 0)
    def _():
        acc_ref[...] = jnp.zeros_like(acc_ref)
        gram_acc_ref[...] = jnp.zeros_like(gram_acc_ref)
        tail_acc_ref[...] = jnp.zeros_like(tail_acc_ref)

    factor = jnp.where(i < STEPS, own_ref[...], other_ref[...])
    high = factor.astype(jnp.bfloat16)
    rest = factor - high.astype(jnp.float32)
    middle, low = split2(rest)
    pair = jnp.concatenate([high, middle], axis=1)
    combined = grad_ref[...].astype(jnp.float32) + error_ref[...]
    top_high, top_low = split2(combined[0])
    bottom_high, bottom_low = split2(combined[1])
    acc_ref[...] += mm_t(pair, jnp.concatenate([top_high, bottom_high], axis=1)) + mm_t(pair, jnp.concatenate([top_low, bottom_low], axis=1))
    gram_acc_ref[...] += mm_t(pair, pair)
    tail_acc_ref[...] += mm_t(high, low)

    @pl.when(i == 2 * STEPS - 1)
    def _():
        right = acc_ref[0:128, :] + acc_ref[128:256, :]
        right_ref[...] = right[0:64, 0:128] + right[64:128, 128:256]
        cross = gram_acc_ref[0:128, 128:256] + tail_acc_ref[...]
        gram = gram_acc_ref[0:128, 0:128] + gram_acc_ref[128:256, 128:256] + (cross + cross.T)
        gram_ref[...] = gram[0:64, 0:64] + gram[64:128, 64:128]


def right_terms(half, grad, error, own, other):
    rows = pl.BlockSpec((2, BLOCK, COLS), both_halves)
    return pl.pallas_call(
        right_kernel,
        out_shape=(jax.ShapeDtypeStruct((RANK, COLS), jnp.float32), jax.ShapeDtypeStruct((RANK, RANK), jnp.float32)),
        grid_spec=pltpu.PrefetchScalarGridSpec(
            num_scalar_prefetch=1,
            grid=(2 * STEPS,),
            in_specs=[
                rows,
                rows,
                pl.BlockSpec((BLOCK, 128), lambda i, half: (jnp.minimum(i, STEPS - 1), 0)),
                pl.BlockSpec((BLOCK, 128), lambda i, half: (jnp.maximum(i - STEPS, 0), 0)),
            ],
            out_specs=(pl.BlockSpec((RANK, COLS), lambda i, half: (0, 0)), pl.BlockSpec((RANK, RANK), lambda i, half: (0, 0))),
            scratch_shapes=[pltpu.VMEM((256, 256), jnp.float32)] * 2 + [pltpu.VMEM((128, 128), jnp.float32)],
        ),
        compiler_params=pltpu.CompilerParams(vmem_limit_bytes=VMEM_LIMIT),
        cost_estimate=pl.CostEstimate(flops=7 * 2 * HALF * 256 * 256, bytes_accessed=ROWS * COLS * 8, transcendentals=0),
        name="right",
    )(half, grad, error, own, other)


def inverse_kernel(gram_ref, inverse_ref):
    a = jnp.concatenate([gram_ref[...], jnp.eye(RANK, dtype=jnp.float32)], axis=1)
    done = []
    for j in range(RANK):
        if j % 8 == 0 and j:
            a = a[8:]
        k = j % 8
        row = a[k : k + 1, :]
        pivot = a[k : k + 1, j : j + 1]
        done.append(row * lax.rsqrt(pivot))
        if j == RANK - 1:
            break
        column = a[:, j : j + 1] / pivot
        below = lax.broadcasted_iota(jnp.int32, column.shape, 0) > k
        a = a - jnp.where(below, column, 0.0) * row
    inverse_ref[...] = jnp.concatenate(done, axis=0)[:, RANK:]


def inverse_lower(gram):
    return pl.pallas_call(
        inverse_kernel,
        out_shape=jax.ShapeDtypeStruct((RANK, RANK), jnp.float32),
        compiler_params=pltpu.CompilerParams(vmem_limit_bytes=VMEM_LIMIT),
        cost_estimate=pl.CostEstimate(flops=RANK**3, bytes_accessed=RANK * RANK * 8, transcendentals=RANK),
        name="inverse",
    )(gram)


def final_kernel(half_ref, grad_ref, error_ref, own_ref, other_ref, right_ref, inverse_ref, update_ref, residual_ref, new_q_ref, high_ref, low_ref):
    i = pl.program_id(0)

    @pl.when(i == 0)
    def _():
        new_q_t = mm_highest(inverse_ref[...], right_ref[...]) * (1.0 / REPLICAS)
        new_q_ref[...] = new_q_t.T
        mixed = mm_highest(inverse_ref[...], new_q_t, ((0,), (0,)))
        for ref, part in zip((high_ref, low_ref), split2(mixed)):
            none = jnp.zeros_like(part)
            two = jnp.concatenate([jnp.concatenate([part, none], axis=1), jnp.concatenate([none, part], axis=1)], axis=0)
            ref[...] = jnp.concatenate([two, two], axis=0)

    factor = jnp.where(i < STEPS, own_ref[...], other_ref[...])
    pair = jnp.concatenate(split2(factor), axis=1)
    wide = mm(pair, high_ref[...]) + mm(pair, low_ref[...])
    for part in range(2):
        lowrank = wide[:, part * 128 : part * 128 + 128]
        update_ref[part] = lowrank.astype(jnp.bfloat16)
        residual_ref[part] = grad_ref[part].astype(jnp.float32) + error_ref[part] - lowrank


def final(half, grad, error, own, other, right, inverse):
    rows = pl.BlockSpec((2, BLOCK, COLS), both_halves)
    return pl.pallas_call(
        final_kernel,
        out_shape=(
            jax.ShapeDtypeStruct((2, ROWS // 2, COLS), jnp.bfloat16),
            jax.ShapeDtypeStruct((2, ROWS // 2, COLS), jnp.float32),
            jax.ShapeDtypeStruct((COLS, RANK), jnp.float32),
        ),
        grid_spec=pltpu.PrefetchScalarGridSpec(
            num_scalar_prefetch=1,
            grid=(2 * STEPS,),
            in_specs=[
                rows,
                rows,
                pl.BlockSpec((BLOCK, 128), lambda i, half: (jnp.minimum(i, STEPS - 1), 0)),
                pl.BlockSpec((BLOCK, 128), lambda i, half: (jnp.maximum(i - STEPS, 0), 0)),
                pl.BlockSpec((RANK, COLS), lambda i, half: (0, 0)),
                pl.BlockSpec((RANK, RANK), lambda i, half: (0, 0)),
            ],
            out_specs=(rows, rows, pl.BlockSpec((COLS, RANK), lambda i, half: (0, 0))),
            scratch_shapes=[pltpu.VMEM((256, 256), jnp.bfloat16)] * 2,
        ),
        compiler_params=pltpu.CompilerParams(vmem_limit_bytes=VMEM_LIMIT),
        cost_estimate=pl.CostEstimate(flops=2 * 2 * HALF * 256 * 256 * 2, bytes_accessed=ROWS * COLS * 14, transcendentals=0),
        name="final",
    )(half, grad, error, own, other, right, inverse)


def swap(a):
    return lax.ppermute(a, "c", [(0, 1), (1, 0)])


def scatter_sum(a, axes, count):
    return lax.all_to_all(a, axes, 0, 0, tiled=True).reshape(count, -1, 128).sum(0)


def gather(a, axes, count):
    return lax.all_to_all(jnp.tile(a, (count, 1)), axes, 0, 0, tiled=True)


def sum_over_replicas(a):
    a = a + swap(a)
    for axis in ("y", "x"):
        for pairs in (PAIR_A, PAIR_B):
            a = a + lax.ppermute(a, axis, pairs)
    return a


def shards(grad, error, warm_q):
    grad = grad.reshape(2, ROWS // 2, COLS)
    error = error.reshape(2, ROWS // 2, COLS)
    half = lax.axis_index("c").astype(jnp.int32).reshape(1)
    away = left_half(1 - half, grad, error, warm_q)
    keep = left_half(half, grad, error, warm_q)
    piece = scatter_sum(keep + swap(away), ("x", "y"), 16)
    piece = scatter_sum(piece, "z", 8)
    own = gather(gather(piece, "z", 8), ("x", "y"), 16)
    other = swap(own)
    right, gram = right_terms(half, grad, error, own, other)
    inverse = inverse_lower(gram)
    right = sum_over_replicas(right)
    update, residual, new_q = final(half, grad, error, own, other, right, inverse)
    return update.reshape(ROWS, COLS), residual.reshape(1, ROWS, COLS), new_q


def solution(mesh):
    grid = Mesh(mesh.devices.reshape(4, 4, 2, 8), ("x", "y", "c", "z"))
    replicas = ("x", "y", "c")
    return jax.shard_map(
        shards,
        mesh=grid,
        in_specs=(P(replicas, None, "z"), P(replicas, None, "z"), P("z", None)),
        out_specs=(P(None, "z"), P(replicas, None, "z"), P("z", None)),
        check_vma=False,
    )
```

```python
import jax
import jax.numpy as jnp
from jax import lax
from jax.experimental import pallas as pl
from jax.experimental.pallas import tpu as pltpu
from jax.sharding import Mesh, PartitionSpec as P

ROWS = 8192
COLS = 128
RANK = 64
HALF = ROWS // 4
BLOCK = 512
STEPS = HALF // BLOCK
REPLICAS = 32
PAIR_A = [(0, 1), (1, 0), (2, 3), (3, 2)]
PAIR_B = [(1, 2), (2, 1), (3, 0), (0, 3)]
RIGHT_BLOCK = 512
VMEM_LIMIT = 24 * 1024 * 1024
LEFT_VMEM_LIMIT = 51 * 1024 * 1024


def split2(a):
    high = a.astype(jnp.bfloat16)
    low = (a - high.astype(jnp.float32)).astype(jnp.bfloat16)
    return high, low


def mm(a, b):
    return jnp.dot(a, b, preferred_element_type=jnp.float32)


def mm_t(a, b):
    return lax.dot_general(a, b, (((0,), (0,)), ((), ())), preferred_element_type=jnp.float32)


def mm_highest(a, b, dims=((1,), (0,))):
    return lax.dot_general(a, b, (dims, ((), ())), precision=lax.Precision.HIGHEST, preferred_element_type=jnp.float32)


def left_kernel(half_ref, grad_ref, error_ref, warm_ref, term_ref, warm_buf, grad_buf, error_buf, warm_sem, grad_sems, error_sems):
    start = pl.multiple_of(half_ref[0] * HALF, HALF)
    warm_copy = pltpu.make_async_copy(warm_ref, warm_buf, warm_sem)
    warm_copy.start()
    copies = []
    for k in range(STEPS):
        source, rows = pl.ds(start + k * BLOCK, BLOCK), pl.ds(k * BLOCK, BLOCK)
        pair = (
            pltpu.make_async_copy(grad_ref.at[:, source, :], grad_buf.at[:, rows, :], grad_sems.at[k]),
            pltpu.make_async_copy(error_ref.at[:, source, :], error_buf.at[:, rows, :], error_sems.at[k]),
        )
        for copy in pair:
            copy.start()
        copies.append(pair)
    warm_copy.wait()
    high, low = split2(warm_buf[...].T)
    none = jnp.zeros_like(high)
    top_right = jnp.concatenate([high, none, low, none], axis=1)
    bottom_right = jnp.concatenate([none, high, none, low], axis=1)
    top_right = jnp.concatenate([top_right, top_right], axis=0)
    bottom_right = jnp.concatenate([bottom_right, bottom_right], axis=0)
    for k in range(STEPS):
        for copy in copies[k]:
            copy.wait()
        rows = pl.ds(k * BLOCK, BLOCK)
        combined = grad_buf[:, rows, :].astype(jnp.float32) + error_buf[:, rows, :]
        top = jnp.concatenate(split2(combined[0]), axis=1)
        bottom = jnp.concatenate(split2(combined[1]), axis=1)
        wide = mm(top, top_right) + mm(bottom, bottom_right)
        term_ref[rows, :] = wide[:, :128] + wide[:, 128:]


SMEM = pl.BlockSpec(memory_space=pltpu.SMEM)
HBM = pl.BlockSpec(memory_space=pltpu.HBM)
VMEM = pl.BlockSpec(memory_space=pltpu.VMEM)


def left_half(half, grad, error, warm_t):
    return pl.pallas_call(
        left_kernel,
        out_shape=jax.ShapeDtypeStruct((HALF, 128), jnp.float32),
        in_specs=[SMEM, HBM, HBM, HBM],
        out_specs=VMEM,
        scratch_shapes=[
            pltpu.VMEM((RANK, COLS), jnp.float32),
            pltpu.VMEM((2, HALF, COLS), jnp.bfloat16),
            pltpu.VMEM((2, HALF, COLS), jnp.float32),
            pltpu.SemaphoreType.DMA,
            pltpu.SemaphoreType.DMA((STEPS,)),
            pltpu.SemaphoreType.DMA((STEPS,)),
        ],
        compiler_params=pltpu.CompilerParams(vmem_limit_bytes=LEFT_VMEM_LIMIT),
        cost_estimate=pl.CostEstimate(flops=2 * 2 * HALF * 256 * 256, bytes_accessed=2 * HALF * COLS * 6, transcendentals=0),
        name="left",
    )(half, grad, error, warm_t)


def rows_of(side, offset):
    return pl.ds(pl.multiple_of(side * HALF + offset, RIGHT_BLOCK), RIGHT_BLOCK)


def add_half(side, grad_ref, error_ref, factor_ref, acc_ref, gram_ref, tail_ref):
    @pl.loop(0, HALF, step=RIGHT_BLOCK)
    def _(start):
        rows = pl.ds(pl.multiple_of(start, RIGHT_BLOCK), RIGHT_BLOCK)
        factor = factor_ref[rows, :]
        high = factor.astype(jnp.bfloat16)
        middle, low = split2(factor - high.astype(jnp.float32))
        pair = jnp.concatenate([high, middle], axis=1)
        source = rows_of(side, start)
        combined = grad_ref[:, source, :].astype(jnp.float32) + error_ref[:, source, :]
        top_high, top_low = split2(combined[0])
        bottom_high, bottom_low = split2(combined[1])
        acc_ref[...] += mm_t(pair, jnp.concatenate([top_high, bottom_high], axis=1)) + mm_t(pair, jnp.concatenate([top_low, bottom_low], axis=1))
        gram_ref[...] += mm_t(pair, pair)
        tail_ref[...] += mm_t(high, low)


def right_own_kernel(half_ref, grad_ref, error_ref, factor_ref, acc_ref, gram_ref, tail_ref):
    for ref in (acc_ref, gram_ref, tail_ref):
        ref[...] = jnp.zeros_like(ref)
    add_half(half_ref[0], grad_ref, error_ref, factor_ref, acc_ref, gram_ref, tail_ref)


def right_other_kernel(half_ref, grad_ref, error_ref, factor_ref, acc_in, gram_in, tail_in, right_ref, gram_ref, acc_ref, gram_acc_ref, tail_acc_ref):
    for ref, given in ((acc_ref, acc_in), (gram_acc_ref, gram_in), (tail_acc_ref, tail_in)):
        ref[...] = given[...]
    add_half(1 - half_ref[0], grad_ref, error_ref, factor_ref, acc_ref, gram_acc_ref, tail_acc_ref)
    right = acc_ref[0:128, :] + acc_ref[128:256, :]
    right_ref[...] = right[0:64, 0:128] + right[64:128, 128:256]
    cross = gram_acc_ref[0:128, 128:256] + tail_acc_ref[...]
    gram = gram_acc_ref[0:128, 0:128] + gram_acc_ref[128:256, 128:256] + (cross + cross.T)
    gram_ref[...] = gram[0:64, 0:64] + gram[64:128, 64:128]


def right_own(half, grad, error, factor):
    square = jax.ShapeDtypeStruct((256, 256), jnp.float32)
    return pl.pallas_call(
        right_own_kernel,
        out_shape=(square, square, jax.ShapeDtypeStruct((128, 128), jnp.float32)),
        in_specs=[SMEM] + [VMEM] * 3,
        out_specs=(VMEM,) * 3,
        compiler_params=pltpu.CompilerParams(vmem_limit_bytes=VMEM_LIMIT),
        cost_estimate=pl.CostEstimate(flops=7 * HALF * 256 * 256, bytes_accessed=ROWS * COLS * 3, transcendentals=0),
        name="right_own",
    )(half, grad, error, factor)


def right_other(half, grad, error, factor, sums):
    return pl.pallas_call(
        right_other_kernel,
        out_shape=(jax.ShapeDtypeStruct((RANK, COLS), jnp.float32), jax.ShapeDtypeStruct((RANK, RANK), jnp.float32)),
        in_specs=[SMEM] + [VMEM] * 6,
        out_specs=(VMEM, VMEM),
        scratch_shapes=[pltpu.VMEM((256, 256), jnp.float32)] * 2 + [pltpu.VMEM((128, 128), jnp.float32)],
        compiler_params=pltpu.CompilerParams(vmem_limit_bytes=VMEM_LIMIT),
        cost_estimate=pl.CostEstimate(flops=7 * HALF * 256 * 256, bytes_accessed=ROWS * COLS * 3, transcendentals=0),
        name="right_other",
    )(half, grad, error, factor, *sums)


def inverse_kernel(gram_ref, inverse_ref):
    a = jnp.concatenate([gram_ref[...], jnp.eye(RANK, dtype=jnp.float32)], axis=1)
    for panel in range(0, RANK, 8):
        spread = [jnp.broadcast_to(a[:, panel + k : panel + k + 1], a.shape) for k in range(8)]
        row_at = lax.broadcasted_iota(jnp.int32, a.shape, 0)
        for k in range(8):
            pivot = spread[k][k : k + 1, :]
            row = a[k : k + 1, :]
            inverse_ref[panel + k : panel + k + 1, :] = (row * lax.rsqrt(pivot))[:, RANK:]
            ratio = jnp.where(row_at > k, spread[k] * (1.0 / pivot), 0.0)
            a = a - ratio * row
            for later in range(k + 1, 8):
                spread[later] = spread[later] - ratio * spread[later][k : k + 1, :]
        a = a[8:]


def inverse_lower(gram):
    return pl.pallas_call(
        inverse_kernel,
        out_shape=jax.ShapeDtypeStruct((RANK, RANK), jnp.float32),
        compiler_params=pltpu.CompilerParams(vmem_limit_bytes=VMEM_LIMIT),
        cost_estimate=pl.CostEstimate(flops=RANK**3, bytes_accessed=RANK * RANK * 8, transcendentals=RANK),
        name="inverse",
    )(gram)


def final_kernel(half_ref, grad_ref, error_ref, own_ref, other_ref, right_ref, inverse_ref, update_ref, residual_ref, new_q_ref, update_buf, residual_buf, update_sems, residual_sems):
    new_q_t = mm_highest(inverse_ref[...], right_ref[...]) * (1.0 / REPLICAS)
    new_q_ref[...] = new_q_t
    mixed = mm_highest(inverse_ref[...], new_q_t, ((0,), (0,)))
    spread = []
    for part in split2(mixed):
        none = jnp.zeros_like(part)
        two = jnp.concatenate([jnp.concatenate([part, none], axis=1), jnp.concatenate([none, part], axis=1)], axis=0)
        spread.append(jnp.concatenate([two, two], axis=0))
    copies = []
    for h, factor_ref in enumerate((own_ref, other_ref)):
        side = half_ref[0] if h == 0 else 1 - half_ref[0]
        start = pl.multiple_of(side * HALF, HALF)
        for k in range(STEPS):
            rows, held, n = pl.ds(k * BLOCK, BLOCK), pl.ds(h * HALF + k * BLOCK, BLOCK), h * STEPS + k
            target = pl.ds(start + k * BLOCK, BLOCK)
            pair = jnp.concatenate(split2(factor_ref[rows, :]), axis=1)
            wide = mm(pair, spread[0]) + mm(pair, spread[1])
            for part in range(2):
                lowrank = wide[:, part * 128 : part * 128 + 128]
                update_buf[part, held, :] = lowrank.astype(jnp.bfloat16)
                residual_buf[part, held, :] = grad_ref[part, target, :].astype(jnp.float32) + error_ref[part, target, :] - lowrank
            for copy in (
                pltpu.make_async_copy(update_buf.at[:, held, :], update_ref.at[:, target, :], update_sems.at[n]),
                pltpu.make_async_copy(residual_buf.at[:, held, :], residual_ref.at[:, target, :], residual_sems.at[n]),
            ):
                copy.start()
                copies.append(copy)
    for copy in copies:
        copy.wait()


def final(half, grad, error, own, other, right, inverse):
    return pl.pallas_call(
        final_kernel,
        out_shape=(
            jax.ShapeDtypeStruct((2, ROWS // 2, COLS), jnp.bfloat16),
            jax.ShapeDtypeStruct((2, ROWS // 2, COLS), jnp.float32),
            jax.ShapeDtypeStruct((RANK, COLS), jnp.float32),
        ),
        in_specs=[SMEM] + [VMEM] * 6,
        out_specs=(HBM, HBM, VMEM),
        scratch_shapes=[
            pltpu.VMEM((2, ROWS // 2, COLS), jnp.bfloat16),
            pltpu.VMEM((2, ROWS // 2, COLS), jnp.float32),
            pltpu.SemaphoreType.DMA((2 * STEPS,)),
            pltpu.SemaphoreType.DMA((2 * STEPS,)),
        ],
        compiler_params=pltpu.CompilerParams(vmem_limit_bytes=VMEM_LIMIT),
        cost_estimate=pl.CostEstimate(flops=2 * 2 * HALF * 256 * 256 * 2, bytes_accessed=ROWS * COLS * 6, transcendentals=0),
        name="final",
    )(half, grad, error, own, other, right, inverse)


def swap(a):
    return lax.ppermute(a, "c", [(0, 1), (1, 0)])


def scatter_sum(a, axes, count):
    return lax.all_to_all(a, axes, 0, 0, tiled=True).reshape(count, -1, 128).sum(0)


def gather(a, axes, count):
    return lax.all_to_all(jnp.tile(a, (count, 1)), axes, 0, 0, tiled=True)


def sum_over_replicas(a):
    a = a + swap(a)
    for axis in ("y", "x"):
        for pairs in (PAIR_A, PAIR_B):
            a = a + lax.ppermute(a, axis, pairs)
    return a


def sum_over_ring8(a):
    inner = [(i, i ^ 1) for i in range(8)]
    outer = [(i, (i + 1) % 8 if i % 2 else (i - 1) % 8) for i in range(8)]
    pair = a + lax.ppermute(a, "z", inner)
    near = lax.ppermute(pair, "z", outer)
    far = lax.ppermute(near, "z", inner)
    opposite = lax.ppermute(far, "z", outer)
    return (pair + near) + (far + opposite)


def shards(grad, error, warm_q):
    grad = grad.reshape(2, ROWS // 2, COLS)
    error = error.reshape(2, ROWS // 2, COLS)
    warm_t = warm_q.T
    half = lax.axis_index("c").astype(jnp.int32).reshape(1)
    away = left_half(1 - half, grad, error, warm_t)
    keep = left_half(half, grad, error, warm_t)
    piece = scatter_sum(keep + swap(away), ("x", "y"), 16)
    piece = sum_over_ring8(piece)
    own = gather(piece, ("x", "y"), 16)
    other = swap(own)
    sums = right_own(half, grad, error, own)
    right, gram = right_other(half, grad, error, other, sums)
    inverse = inverse_lower(gram)
    right = sum_over_replicas(right)
    update, residual, new_q_t = final(half, grad, error, own, other, right, inverse)
    return update.reshape(ROWS, COLS), residual.reshape(1, ROWS, COLS), new_q_t.T


def solution(mesh):
    grid = Mesh(mesh.devices.reshape(4, 4, 2, 8), ("x", "y", "c", "z"))
    replicas = ("x", "y", "c")
    return jax.shard_map(
        shards,
        mesh=grid,
        in_specs=(P(replicas, None, "z"), P(replicas, None, "z"), P("z", None)),
        out_specs=(P(None, "z"), P(replicas, None, "z"), P("z", None)),
        check_vma=False,
    )
```

```python
import jax
import jax.numpy as jnp
from jax import lax
from jax.experimental import pallas as pl
from jax.experimental.pallas import tpu as pltpu
from jax.sharding import Mesh, PartitionSpec as P

ROWS = 8192
COLS = 128
RANK = 64
HALF = ROWS // 4
BLOCK = 512
STEPS = HALF // BLOCK
REPLICAS = 32
PAIR_A = [(0, 1), (1, 0), (2, 3), (3, 2)]
PAIR_B = [(1, 2), (2, 1), (3, 0), (0, 3)]
RIGHT_BLOCK = 512
VMEM_LIMIT = 24 * 1024 * 1024
LEFT_VMEM_LIMIT = 51 * 1024 * 1024


def split2(a):
    high = a.astype(jnp.bfloat16)
    low = (a - high.astype(jnp.float32)).astype(jnp.bfloat16)
    return high, low


def mm(a, b):
    return jnp.dot(a, b, preferred_element_type=jnp.float32)


def mm_t(a, b):
    return lax.dot_general(a, b, (((0,), (0,)), ((), ())), preferred_element_type=jnp.float32)


def mm_highest(a, b, dims=((1,), (0,))):
    return lax.dot_general(a, b, (dims, ((), ())), precision=lax.Precision.HIGHEST, preferred_element_type=jnp.float32)


def left_kernel(half_ref, grad_ref, error_ref, warm_ref, term_ref, warm_buf, grad_buf, error_buf, warm_sem, grad_sems, error_sems):
    start = pl.multiple_of(half_ref[0] * HALF, HALF)
    warm_copy = pltpu.make_async_copy(warm_ref, warm_buf, warm_sem)
    warm_copy.start()
    copies = []
    for k in range(STEPS):
        source, rows = pl.ds(start + k * BLOCK, BLOCK), pl.ds(k * BLOCK, BLOCK)
        pair = (
            pltpu.make_async_copy(grad_ref.at[:, source, :], grad_buf.at[:, rows, :], grad_sems.at[k]),
            pltpu.make_async_copy(error_ref.at[:, source, :], error_buf.at[:, rows, :], error_sems.at[k]),
        )
        for copy in pair:
            copy.start()
        copies.append(pair)
    warm_copy.wait()
    high, low = split2(warm_buf[...].T)
    none = jnp.zeros_like(high)
    top_right = jnp.concatenate([high, none, low, none], axis=1)
    bottom_right = jnp.concatenate([none, high, none, low], axis=1)
    top_right = jnp.concatenate([top_right, top_right], axis=0)
    bottom_right = jnp.concatenate([bottom_right, bottom_right], axis=0)
    for k in range(STEPS):
        for copy in copies[k]:
            copy.wait()
        rows = pl.ds(k * BLOCK, BLOCK)
        combined = grad_buf[:, rows, :].astype(jnp.float32) + error_buf[:, rows, :]
        top = jnp.concatenate(split2(combined[0]), axis=1)
        bottom = jnp.concatenate(split2(combined[1]), axis=1)
        wide = mm(top, top_right) + mm(bottom, bottom_right)
        term_ref[rows, :] = wide[:, :128] + wide[:, 128:]


SMEM = pl.BlockSpec(memory_space=pltpu.SMEM)
HBM = pl.BlockSpec(memory_space=pltpu.HBM)
VMEM = pl.BlockSpec(memory_space=pltpu.VMEM)


def left_half(half, grad, error, warm_t):
    return pl.pallas_call(
        left_kernel,
        out_shape=jax.ShapeDtypeStruct((HALF, 128), jnp.float32),
        in_specs=[SMEM, HBM, HBM, HBM],
        out_specs=VMEM,
        scratch_shapes=[
            pltpu.VMEM((RANK, COLS), jnp.float32),
            pltpu.VMEM((2, HALF, COLS), jnp.bfloat16),
            pltpu.VMEM((2, HALF, COLS), jnp.float32),
            pltpu.SemaphoreType.DMA,
            pltpu.SemaphoreType.DMA((STEPS,)),
            pltpu.SemaphoreType.DMA((STEPS,)),
        ],
        compiler_params=pltpu.CompilerParams(vmem_limit_bytes=LEFT_VMEM_LIMIT),
        cost_estimate=pl.CostEstimate(flops=2 * 2 * HALF * 256 * 256, bytes_accessed=2 * HALF * COLS * 6, transcendentals=0),
        name="left",
    )(half, grad, error, warm_t)


def add_half(combined_ref, factor_ref, acc_ref, gram_ref, tail_ref):
    @pl.loop(0, HALF, step=RIGHT_BLOCK)
    def _(start):
        rows = pl.ds(pl.multiple_of(start, RIGHT_BLOCK), RIGHT_BLOCK)
        factor = factor_ref[rows, :]
        high = factor.astype(jnp.bfloat16)
        middle, low = split2(factor - high.astype(jnp.float32))
        pair = jnp.concatenate([high, middle], axis=1)
        top_high, top_low = split2(combined_ref[0, rows, :])
        bottom_high, bottom_low = split2(combined_ref[1, rows, :])
        acc_ref[...] += mm_t(pair, jnp.concatenate([top_high, bottom_high], axis=1)) + mm_t(pair, jnp.concatenate([top_low, bottom_low], axis=1))
        gram_ref[...] += mm_t(pair, pair)
        tail_ref[...] += mm_t(high, low)


def right_own_kernel(combined_ref, factor_ref, acc_ref, gram_ref, tail_ref):
    for ref in (acc_ref, gram_ref, tail_ref):
        ref[...] = jnp.zeros_like(ref)
    add_half(combined_ref, factor_ref, acc_ref, gram_ref, tail_ref)


def right_other_kernel(combined_ref, factor_ref, acc_in, gram_in, tail_in, right_ref, gram_ref, acc_ref, gram_acc_ref, tail_acc_ref):
    for ref, given in ((acc_ref, acc_in), (gram_acc_ref, gram_in), (tail_acc_ref, tail_in)):
        ref[...] = given[...]
    add_half(combined_ref, factor_ref, acc_ref, gram_acc_ref, tail_acc_ref)
    right = acc_ref[0:128, :] + acc_ref[128:256, :]
    right_ref[...] = right[0:64, 0:128] + right[64:128, 128:256]
    cross = gram_acc_ref[0:128, 128:256] + tail_acc_ref[...]
    gram = gram_acc_ref[0:128, 0:128] + gram_acc_ref[128:256, 128:256] + (cross + cross.T)
    gram_ref[...] = gram[0:64, 0:64] + gram[64:128, 64:128]


def right_own(combined, factor):
    square = jax.ShapeDtypeStruct((256, 256), jnp.float32)
    return pl.pallas_call(
        right_own_kernel,
        out_shape=(square, square, jax.ShapeDtypeStruct((128, 128), jnp.float32)),
        in_specs=[VMEM] * 2,
        out_specs=(VMEM,) * 3,
        compiler_params=pltpu.CompilerParams(vmem_limit_bytes=VMEM_LIMIT),
        cost_estimate=pl.CostEstimate(flops=7 * HALF * 256 * 256, bytes_accessed=ROWS * COLS * 3, transcendentals=0),
        name="right_own",
    )(combined, factor)


def right_other(combined, factor, sums):
    return pl.pallas_call(
        right_other_kernel,
        out_shape=(jax.ShapeDtypeStruct((RANK, COLS), jnp.float32), jax.ShapeDtypeStruct((RANK, RANK), jnp.float32)),
        in_specs=[VMEM] * 5,
        out_specs=(VMEM, VMEM),
        scratch_shapes=[pltpu.VMEM((256, 256), jnp.float32)] * 2 + [pltpu.VMEM((128, 128), jnp.float32)],
        compiler_params=pltpu.CompilerParams(vmem_limit_bytes=VMEM_LIMIT),
        cost_estimate=pl.CostEstimate(flops=7 * HALF * 256 * 256, bytes_accessed=ROWS * COLS * 3, transcendentals=0),
        name="right_other",
    )(combined, factor, *sums)


def inverse_kernel(gram_ref, inverse_ref):
    a = jnp.concatenate([gram_ref[...], jnp.eye(RANK, dtype=jnp.float32)], axis=1)
    for panel in range(0, RANK, 8):
        spread = [jnp.broadcast_to(a[:, panel + k : panel + k + 1], a.shape) for k in range(8)]
        row_at = lax.broadcasted_iota(jnp.int32, a.shape, 0)
        for k in range(8):
            pivot = spread[k][k : k + 1, :]
            row = a[k : k + 1, :]
            inverse_ref[panel + k : panel + k + 1, :] = (row * lax.rsqrt(pivot))[:, RANK:]
            ratio = jnp.where(row_at > k, spread[k] * (1.0 / pivot), 0.0)
            a = a - ratio * row
            for later in range(k + 1, 8):
                spread[later] = spread[later] - ratio * spread[later][k : k + 1, :]
        a = a[8:]


def inverse_lower(gram):
    return pl.pallas_call(
        inverse_kernel,
        out_shape=jax.ShapeDtypeStruct((RANK, RANK), jnp.float32),
        compiler_params=pltpu.CompilerParams(vmem_limit_bytes=VMEM_LIMIT),
        cost_estimate=pl.CostEstimate(flops=RANK**3, bytes_accessed=RANK * RANK * 8, transcendentals=RANK),
        name="inverse",
    )(gram)


def final_kernel(half_ref, own_combined_ref, other_combined_ref, own_ref, other_ref, right_ref, inverse_ref, update_ref, residual_ref, new_q_ref, update_buf, residual_buf, update_sems, residual_sems):
    new_q_t = mm_highest(inverse_ref[...], right_ref[...]) * (1.0 / REPLICAS)
    new_q_ref[...] = new_q_t
    mixed = mm_highest(inverse_ref[...], new_q_t, ((0,), (0,)))
    spread = []
    for part in split2(mixed):
        none = jnp.zeros_like(part)
        two = jnp.concatenate([jnp.concatenate([part, none], axis=1), jnp.concatenate([none, part], axis=1)], axis=0)
        spread.append(jnp.concatenate([two, two], axis=0))
    copies = []
    for h, (combined_ref, factor_ref) in enumerate(((own_combined_ref, own_ref), (other_combined_ref, other_ref))):
        side = half_ref[0] if h == 0 else 1 - half_ref[0]
        start = pl.multiple_of(side * HALF, HALF)
        for k in range(STEPS):
            rows, held, n = pl.ds(k * BLOCK, BLOCK), pl.ds(h * HALF + k * BLOCK, BLOCK), h * STEPS + k
            target = pl.ds(start + k * BLOCK, BLOCK)
            pair = jnp.concatenate(split2(factor_ref[rows, :]), axis=1)
            wide = mm(pair, spread[0]) + mm(pair, spread[1])
            for part in range(2):
                lowrank = wide[:, part * 128 : part * 128 + 128]
                update_buf[part, held, :] = lowrank.astype(jnp.bfloat16)
                residual_buf[part, held, :] = combined_ref[part, rows, :] - lowrank
            for copy in (
                pltpu.make_async_copy(update_buf.at[:, held, :], update_ref.at[:, target, :], update_sems.at[n]),
                pltpu.make_async_copy(residual_buf.at[:, held, :], residual_ref.at[:, target, :], residual_sems.at[n]),
            ):
                copy.start()
                copies.append(copy)
    for copy in copies:
        copy.wait()


def final(half, own_combined, other_combined, own, other, right, inverse):
    return pl.pallas_call(
        final_kernel,
        out_shape=(
            jax.ShapeDtypeStruct((2, ROWS // 2, COLS), jnp.bfloat16),
            jax.ShapeDtypeStruct((2, ROWS // 2, COLS), jnp.float32),
            jax.ShapeDtypeStruct((RANK, COLS), jnp.float32),
        ),
        in_specs=[SMEM] + [VMEM] * 6,
        out_specs=(HBM, HBM, VMEM),
        scratch_shapes=[
            pltpu.VMEM((2, ROWS // 2, COLS), jnp.bfloat16),
            pltpu.VMEM((2, ROWS // 2, COLS), jnp.float32),
            pltpu.SemaphoreType.DMA((2 * STEPS,)),
            pltpu.SemaphoreType.DMA((2 * STEPS,)),
        ],
        compiler_params=pltpu.CompilerParams(vmem_limit_bytes=VMEM_LIMIT),
        cost_estimate=pl.CostEstimate(flops=2 * 2 * HALF * 256 * 256 * 2, bytes_accessed=ROWS * COLS * 6, transcendentals=0),
        name="final",
    )(half, own_combined, other_combined, own, other, right, inverse)


def swap(a):
    return lax.ppermute(a, "c", [(0, 1), (1, 0)])


def scatter_sum(a, axes, count):
    return lax.all_to_all(a, axes, 0, 0, tiled=True).reshape(count, -1, 128).sum(0)


def gather(a, axes, count):
    return lax.all_to_all(jnp.tile(a, (count, 1)), axes, 0, 0, tiled=True)


def sum_over_replicas(a, gram):
    a = a + swap(a)
    for axis in ("y", "x"):
        for pairs in (PAIR_A, PAIR_B):
            a = a + lax.ppermute(a, axis, pairs)
        if axis == "y":
            a, inverse = lax.optimization_barrier((a, inverse_lower(gram)))
    return a, inverse


def combined_half(grad, error, half):
    start = half[0] * HALF
    part = (2, HALF, COLS)
    return lax.dynamic_slice(grad, (0, start, 0), part).astype(jnp.float32) + lax.dynamic_slice(error, (0, start, 0), part)


RING_A = [(i, i ^ 1) for i in range(8)]
RING_B = [(i, (i + 1) % 8 if i % 2 else (i - 1) % 8) for i in range(8)]


def shards(grad, error, warm_q):
    grad = grad.reshape(2, ROWS // 2, COLS)
    error = error.reshape(2, ROWS // 2, COLS)
    warm_t = warm_q.T
    half = lax.axis_index("c").astype(jnp.int32).reshape(1)
    away = left_half(1 - half, grad, error, warm_t)
    keep = left_half(half, grad, error, warm_t)
    piece = scatter_sum(keep + swap(away), ("x", "y"), 16)
    pair = piece + lax.ppermute(piece, "z", RING_A)
    pair, grad, error = lax.optimization_barrier((pair, grad, error))
    near = lax.ppermute(pair, "z", RING_B)
    near, own_combined, grad, error = lax.optimization_barrier((near, combined_half(grad, error, half), grad, error))
    far = lax.ppermute(near, "z", RING_A)
    far, other_combined = lax.optimization_barrier((far, combined_half(grad, error, 1 - half)))
    opposite = lax.ppermute(far, "z", RING_B)
    piece = (pair + near) + (far + opposite)
    own = gather(piece, ("x", "y"), 16)
    other = swap(own)
    sums = right_own(own_combined, own)
    right, gram = right_other(other_combined, other, sums)
    right, inverse = sum_over_replicas(right, gram)
    update, residual, new_q_t = final(half, own_combined, other_combined, own, other, right, inverse)
    return update.reshape(ROWS, COLS), residual.reshape(1, ROWS, COLS), new_q_t.T


def solution(mesh):
    grid = Mesh(mesh.devices.reshape(4, 4, 2, 8), ("x", "y", "c", "z"))
    replicas = ("x", "y", "c")
    return jax.shard_map(
        shards,
        mesh=grid,
        in_specs=(P(replicas, None, "z"), P(replicas, None, "z"), P("z", None)),
        out_specs=(P(None, "z"), P(replicas, None, "z"), P("z", None)),
        check_vma=False,
    )
```

```python
import jax
import jax.numpy as jnp
from jax import lax
from jax.experimental import pallas as pl
from jax.experimental.pallas import tpu as pltpu
from jax.sharding import Mesh, PartitionSpec as P

ROWS = 8192
COLS = 128
RANK = 64
HALF = ROWS // 4
BLOCK = 512
STEPS = HALF // BLOCK
REPLICAS = 32
PAIR_A = [(0, 1), (1, 0), (2, 3), (3, 2)]
PAIR_B = [(1, 2), (2, 1), (3, 0), (0, 3)]
LEFT_BLOCK = 1024
LEFT_STEPS = HALF // LEFT_BLOCK
RIGHT_BLOCK = 512
VMEM_LIMIT = 24 * 1024 * 1024
LEFT_VMEM_LIMIT = 51 * 1024 * 1024


def split2(a):
    high = a.astype(jnp.bfloat16)
    low = (a - high.astype(jnp.float32)).astype(jnp.bfloat16)
    return high, low


def mm(a, b):
    return jnp.dot(a, b, preferred_element_type=jnp.float32)


def mm_t(a, b):
    return lax.dot_general(a, b, (((0,), (0,)), ((), ())), preferred_element_type=jnp.float32)


def mm_highest(a, b, dims=((1,), (0,))):
    return lax.dot_general(a, b, (dims, ((), ())), precision=lax.Precision.HIGHEST, preferred_element_type=jnp.float32)


def left_kernel(half_ref, grad_ref, error_ref, warm_ref, term_ref, warm_buf, grad_buf, error_buf, warm_sem, grad_sems, error_sems):
    start = pl.multiple_of(half_ref[0] * HALF, HALF)
    warm_copy = pltpu.make_async_copy(warm_ref, warm_buf, warm_sem)
    warm_copy.start()
    copies = []
    for k in range(LEFT_STEPS):
        source, rows = pl.ds(start + k * LEFT_BLOCK, LEFT_BLOCK), pl.ds(k * LEFT_BLOCK, LEFT_BLOCK)
        pair = (
            pltpu.make_async_copy(grad_ref.at[:, source, :], grad_buf.at[:, rows, :], grad_sems.at[k]),
            pltpu.make_async_copy(error_ref.at[:, source, :], error_buf.at[:, rows, :], error_sems.at[k]),
        )
        for copy in pair:
            copy.start()
        copies.append(pair)
    warm_copy.wait()
    high, low = split2(warm_buf[...].T)
    none = jnp.zeros_like(high)
    top_right = jnp.concatenate([high, none, low, none], axis=1)
    bottom_right = jnp.concatenate([none, high, none, low], axis=1)
    top_right = jnp.concatenate([top_right, top_right], axis=0)
    bottom_right = jnp.concatenate([bottom_right, bottom_right], axis=0)
    for k in range(LEFT_STEPS):
        for copy in copies[k]:
            copy.wait()
        rows = pl.ds(k * LEFT_BLOCK, LEFT_BLOCK)
        combined = grad_buf[:, rows, :].astype(jnp.float32) + error_buf[:, rows, :]
        top = jnp.concatenate(split2(combined[0]), axis=1)
        bottom = jnp.concatenate(split2(combined[1]), axis=1)
        wide = mm(top, top_right) + mm(bottom, bottom_right)
        term_ref[rows, :] = wide[:, :128] + wide[:, 128:]


SMEM = pl.BlockSpec(memory_space=pltpu.SMEM)
HBM = pl.BlockSpec(memory_space=pltpu.HBM)
VMEM = pl.BlockSpec(memory_space=pltpu.VMEM)


def left_half(half, grad, error, warm_t):
    return pl.pallas_call(
        left_kernel,
        out_shape=jax.ShapeDtypeStruct((HALF, 128), jnp.float32),
        in_specs=[SMEM, HBM, HBM, HBM],
        out_specs=VMEM,
        scratch_shapes=[
            pltpu.VMEM((RANK, COLS), jnp.float32),
            pltpu.VMEM((2, HALF, COLS), jnp.bfloat16),
            pltpu.VMEM((2, HALF, COLS), jnp.float32),
            pltpu.SemaphoreType.DMA,
            pltpu.SemaphoreType.DMA((LEFT_STEPS,)),
            pltpu.SemaphoreType.DMA((LEFT_STEPS,)),
        ],
        compiler_params=pltpu.CompilerParams(vmem_limit_bytes=LEFT_VMEM_LIMIT),
        cost_estimate=pl.CostEstimate(flops=2 * 2 * HALF * 256 * 256, bytes_accessed=2 * HALF * COLS * 6, transcendentals=0),
        name="left",
    )(half, grad, error, warm_t)


def add_half(combined_ref, factor_ref, acc_ref, gram_ref, tail_ref):
    @pl.loop(0, HALF, step=RIGHT_BLOCK)
    def _(start):
        rows = pl.ds(pl.multiple_of(start, RIGHT_BLOCK), RIGHT_BLOCK)
        factor = factor_ref[rows, :]
        high = factor.astype(jnp.bfloat16)
        middle, low = split2(factor - high.astype(jnp.float32))
        pair = jnp.concatenate([high, middle], axis=1)
        top_high, top_low = split2(combined_ref[0, rows, :])
        bottom_high, bottom_low = split2(combined_ref[1, rows, :])
        acc_ref[...] += mm_t(pair, jnp.concatenate([top_high, bottom_high], axis=1)) + mm_t(pair, jnp.concatenate([top_low, bottom_low], axis=1))
        gram_ref[...] += mm_t(pair, pair)
        tail_ref[...] += mm_t(high, low)


def right_own_kernel(combined_ref, factor_ref, acc_ref, gram_ref, tail_ref):
    for ref in (acc_ref, gram_ref, tail_ref):
        ref[...] = jnp.zeros_like(ref)
    add_half(combined_ref, factor_ref, acc_ref, gram_ref, tail_ref)


def right_other_kernel(combined_ref, factor_ref, acc_in, gram_in, tail_in, right_ref, gram_ref, acc_ref, gram_acc_ref, tail_acc_ref):
    for ref, given in ((acc_ref, acc_in), (gram_acc_ref, gram_in), (tail_acc_ref, tail_in)):
        ref[...] = given[...]
    add_half(combined_ref, factor_ref, acc_ref, gram_acc_ref, tail_acc_ref)
    right = acc_ref[0:128, :] + acc_ref[128:256, :]
    right_ref[...] = right[0:64, 0:128] + right[64:128, 128:256]
    cross = gram_acc_ref[0:128, 128:256] + tail_acc_ref[...]
    gram = gram_acc_ref[0:128, 0:128] + gram_acc_ref[128:256, 128:256] + (cross + cross.T)
    gram_ref[...] = gram[0:64, 0:64] + gram[64:128, 64:128]


def right_own(combined, factor):
    square = jax.ShapeDtypeStruct((256, 256), jnp.float32)
    return pl.pallas_call(
        right_own_kernel,
        out_shape=(square, square, jax.ShapeDtypeStruct((128, 128), jnp.float32)),
        in_specs=[VMEM] * 2,
        out_specs=(VMEM,) * 3,
        compiler_params=pltpu.CompilerParams(vmem_limit_bytes=VMEM_LIMIT),
        cost_estimate=pl.CostEstimate(flops=7 * HALF * 256 * 256, bytes_accessed=ROWS * COLS * 3, transcendentals=0),
        name="right_own",
    )(combined, factor)


def right_other(combined, factor, sums):
    return pl.pallas_call(
        right_other_kernel,
        out_shape=(jax.ShapeDtypeStruct((RANK, COLS), jnp.float32), jax.ShapeDtypeStruct((RANK, RANK), jnp.float32)),
        in_specs=[VMEM] * 5,
        out_specs=(VMEM, VMEM),
        scratch_shapes=[pltpu.VMEM((256, 256), jnp.float32)] * 2 + [pltpu.VMEM((128, 128), jnp.float32)],
        compiler_params=pltpu.CompilerParams(vmem_limit_bytes=VMEM_LIMIT),
        cost_estimate=pl.CostEstimate(flops=7 * HALF * 256 * 256, bytes_accessed=ROWS * COLS * 3, transcendentals=0),
        name="right_other",
    )(combined, factor, *sums)


def inverse_kernel(gram_ref, inverse_ref):
    a = jnp.concatenate([gram_ref[...], jnp.eye(RANK, dtype=jnp.float32)], axis=1)
    for panel in range(0, RANK, 8):
        spread = [jnp.broadcast_to(a[:, panel + k : panel + k + 1], a.shape) for k in range(8)]
        row_at = lax.broadcasted_iota(jnp.int32, a.shape, 0)
        for k in range(8):
            pivot = spread[k][k : k + 1, :]
            row = a[k : k + 1, :]
            inverse_ref[panel + k : panel + k + 1, :] = (row * lax.rsqrt(pivot))[:, RANK:]
            ratio = jnp.where(row_at > k, spread[k] * (1.0 / pivot), 0.0)
            a = a - ratio * row
            for later in range(k + 1, 8):
                spread[later] = spread[later] - ratio * spread[later][k : k + 1, :]
        a = a[8:]


def inverse_lower(gram):
    return pl.pallas_call(
        inverse_kernel,
        out_shape=jax.ShapeDtypeStruct((RANK, RANK), jnp.float32),
        compiler_params=pltpu.CompilerParams(vmem_limit_bytes=VMEM_LIMIT),
        cost_estimate=pl.CostEstimate(flops=RANK**3, bytes_accessed=RANK * RANK * 8, transcendentals=RANK),
        name="inverse",
    )(gram)


def final_kernel(half_ref, own_combined_ref, other_combined_ref, own_ref, other_ref, right_ref, inverse_ref, update_ref, residual_ref, new_q_ref, update_buf, residual_buf, update_sems, residual_sems):
    new_q_t = mm_highest(inverse_ref[...], right_ref[...]) * (1.0 / REPLICAS)
    new_q_ref[...] = new_q_t
    mixed = mm_highest(inverse_ref[...], new_q_t, ((0,), (0,)))
    spread = []
    for part in split2(mixed):
        none = jnp.zeros_like(part)
        two = jnp.concatenate([jnp.concatenate([part, none], axis=1), jnp.concatenate([none, part], axis=1)], axis=0)
        spread.append(jnp.concatenate([two, two], axis=0))
    copies = []
    for h, (combined_ref, factor_ref) in enumerate(((own_combined_ref, own_ref), (other_combined_ref, other_ref))):
        side = half_ref[0] if h == 0 else 1 - half_ref[0]
        start = pl.multiple_of(side * HALF, HALF)
        for k in range(STEPS):
            rows, held, n = pl.ds(k * BLOCK, BLOCK), pl.ds(h * HALF + k * BLOCK, BLOCK), h * STEPS + k
            target = pl.ds(start + k * BLOCK, BLOCK)
            pair = jnp.concatenate(split2(factor_ref[rows, :]), axis=1)
            wide = mm(pair, spread[0]) + mm(pair, spread[1])
            for part in range(2):
                lowrank = wide[:, part * 128 : part * 128 + 128]
                update_buf[part, held, :] = lowrank.astype(jnp.bfloat16)
                residual_buf[part, held, :] = combined_ref[part, rows, :] - lowrank
            for copy in (
                pltpu.make_async_copy(update_buf.at[:, held, :], update_ref.at[:, target, :], update_sems.at[n]),
                pltpu.make_async_copy(residual_buf.at[:, held, :], residual_ref.at[:, target, :], residual_sems.at[n]),
            ):
                copy.start()
                copies.append(copy)
    for copy in copies:
        copy.wait()


def final(half, own_combined, other_combined, own, other, right, inverse):
    return pl.pallas_call(
        final_kernel,
        out_shape=(
            jax.ShapeDtypeStruct((2, ROWS // 2, COLS), jnp.bfloat16),
            jax.ShapeDtypeStruct((2, ROWS // 2, COLS), jnp.float32),
            jax.ShapeDtypeStruct((RANK, COLS), jnp.float32),
        ),
        in_specs=[SMEM] + [VMEM] * 6,
        out_specs=(HBM, HBM, VMEM),
        scratch_shapes=[
            pltpu.VMEM((2, ROWS // 2, COLS), jnp.bfloat16),
            pltpu.VMEM((2, ROWS // 2, COLS), jnp.float32),
            pltpu.SemaphoreType.DMA((2 * STEPS,)),
            pltpu.SemaphoreType.DMA((2 * STEPS,)),
        ],
        compiler_params=pltpu.CompilerParams(vmem_limit_bytes=VMEM_LIMIT),
        cost_estimate=pl.CostEstimate(flops=2 * 2 * HALF * 256 * 256 * 2, bytes_accessed=ROWS * COLS * 6, transcendentals=0),
        name="final",
    )(half, own_combined, other_combined, own, other, right, inverse)


def swap(a):
    return lax.ppermute(a, "c", [(0, 1), (1, 0)])


def scatter_sum(a, axes, count):
    return lax.all_to_all(a, axes, 0, 0, tiled=True).reshape(count, -1, 128).sum(0)


def gather(a, axes, count):
    return lax.all_to_all(jnp.tile(a, (count, 1)), axes, 0, 0, tiled=True)


def sum_over_replicas(a, gram):
    a = a + swap(a)
    for axis in ("y", "x"):
        for pairs in (PAIR_A, PAIR_B):
            a = a + lax.ppermute(a, (axis, "c"), [(2 * i + c, 2 * j + 1 - c) for i, j in pairs for c in range(2)])
        if axis == "y":
            a, inverse = lax.optimization_barrier((a, inverse_lower(gram)))
    return a, inverse


def combined_half(grad, error, half):
    start = half[0] * HALF
    part = (2, HALF, COLS)
    return lax.dynamic_slice(grad, (0, start, 0), part).astype(jnp.float32) + lax.dynamic_slice(error, (0, start, 0), part)


RING_A = [(i, i ^ 1) for i in range(8)]
RING_B = [(i, (i + 1) % 8 if i % 2 else (i - 1) % 8) for i in range(8)]


def shards(grad, error, warm_q):
    grad = grad.reshape(2, ROWS // 2, COLS)
    error = error.reshape(2, ROWS // 2, COLS)
    warm_t = warm_q.T
    half = lax.axis_index("c").astype(jnp.int32).reshape(1)
    away = left_half(1 - half, grad, error, warm_t)
    keep = left_half(half, grad, error, warm_t)
    piece = scatter_sum(keep + swap(away), ("x", "y"), 16)
    pair = piece + lax.ppermute(piece, "z", RING_A)
    pair, grad, error = lax.optimization_barrier((pair, grad, error))
    near = lax.ppermute(pair, "z", RING_B)
    near, own_combined, grad, error = lax.optimization_barrier((near, combined_half(grad, error, half), grad, error))
    far = lax.ppermute(near, "z", RING_A)
    far, other_combined = lax.optimization_barrier((far, combined_half(grad, error, 1 - half)))
    opposite = lax.ppermute(far, "z", RING_B)
    piece = (pair + near) + (far + opposite)
    own = gather(piece, ("x", "y"), 16)
    other = swap(own)
    sums = right_own(own_combined, own)
    right, gram = right_other(other_combined, other, sums)
    right, inverse = sum_over_replicas(right, gram)
    update, residual, new_q_t = final(half, own_combined, other_combined, own, other, right, inverse)
    return update.reshape(ROWS, COLS), residual.reshape(1, ROWS, COLS), new_q_t.T


def solution(mesh):
    grid = Mesh(mesh.devices.reshape(4, 4, 2, 8), ("x", "y", "c", "z"))
    replicas = ("x", "y", "c")
    return jax.shard_map(
        shards,
        mesh=grid,
        in_specs=(P(replicas, None, "z"), P(replicas, None, "z"), P("z", None)),
        out_specs=(P(None, "z"), P(replicas, None, "z"), P("z", None)),
        check_vma=False,
    )
```

```python
import jax
import jax.numpy as jnp
from jax import lax
from jax.experimental import pallas as pl
from jax.experimental.pallas import tpu as pltpu
from jax.sharding import Mesh, PartitionSpec as P

ROWS = 8192
COLS = 128
RANK = 64
HALF = ROWS // 4
BLOCK = 512
STEPS = HALF // BLOCK
REPLICAS = 32
LEFT_BLOCK = 1024
LEFT_STEPS = HALF // LEFT_BLOCK
RIGHT_BLOCK = 512
VMEM_LIMIT = 24 * 1024 * 1024
LEFT_VMEM_LIMIT = 51 * 1024 * 1024


def split2(a):
    high = a.astype(jnp.bfloat16)
    low = (a - high.astype(jnp.float32)).astype(jnp.bfloat16)
    return high, low


def mm(a, b):
    return jnp.dot(a, b, preferred_element_type=jnp.float32)


def mm_t(a, b):
    return lax.dot_general(a, b, (((0,), (0,)), ((), ())), preferred_element_type=jnp.float32)


def mm_highest(a, b, dims=((1,), (0,))):
    return lax.dot_general(a, b, (dims, ((), ())), precision=lax.Precision.HIGHEST, preferred_element_type=jnp.float32)


def left_kernel(half_ref, grad_ref, error_ref, warm_ref, term_ref, warm_buf, grad_buf, error_buf, warm_sem, grad_sems, error_sems):
    start = pl.multiple_of(half_ref[0] * HALF, HALF)
    warm_copy = pltpu.make_async_copy(warm_ref, warm_buf, warm_sem)
    warm_copy.start()
    copies = []
    for k in range(LEFT_STEPS):
        source, rows = pl.ds(start + k * LEFT_BLOCK, LEFT_BLOCK), pl.ds(k * LEFT_BLOCK, LEFT_BLOCK)
        pair = (
            pltpu.make_async_copy(grad_ref.at[:, source, :], grad_buf.at[:, rows, :], grad_sems.at[k]),
            pltpu.make_async_copy(error_ref.at[:, source, :], error_buf.at[:, rows, :], error_sems.at[k]),
        )
        for copy in pair:
            copy.start()
        copies.append(pair)
    warm_copy.wait()
    high, low = split2(warm_buf[...].T)
    none = jnp.zeros_like(high)
    top_right = jnp.concatenate([high, none, low, none], axis=1)
    bottom_right = jnp.concatenate([none, high, none, low], axis=1)
    top_right = jnp.concatenate([top_right, top_right], axis=0)
    bottom_right = jnp.concatenate([bottom_right, bottom_right], axis=0)
    for k in range(LEFT_STEPS):
        for copy in copies[k]:
            copy.wait()
        rows = pl.ds(k * LEFT_BLOCK, LEFT_BLOCK)
        combined = grad_buf[:, rows, :].astype(jnp.float32) + error_buf[:, rows, :]
        top = jnp.concatenate(split2(combined[0]), axis=1)
        bottom = jnp.concatenate(split2(combined[1]), axis=1)
        wide = mm(top, top_right) + mm(bottom, bottom_right)
        term_ref[rows, :] = wide[:, :128] + wide[:, 128:]


SMEM = pl.BlockSpec(memory_space=pltpu.SMEM)
HBM = pl.BlockSpec(memory_space=pltpu.HBM)
VMEM = pl.BlockSpec(memory_space=pltpu.VMEM)


def left_half(half, grad, error, warm_t):
    return pl.pallas_call(
        left_kernel,
        out_shape=jax.ShapeDtypeStruct((HALF, 128), jnp.float32),
        in_specs=[SMEM, HBM, HBM, HBM],
        out_specs=VMEM,
        scratch_shapes=[
            pltpu.VMEM((RANK, COLS), jnp.float32),
            pltpu.VMEM((2, HALF, COLS), jnp.bfloat16),
            pltpu.VMEM((2, HALF, COLS), jnp.float32),
            pltpu.SemaphoreType.DMA,
            pltpu.SemaphoreType.DMA((LEFT_STEPS,)),
            pltpu.SemaphoreType.DMA((LEFT_STEPS,)),
        ],
        compiler_params=pltpu.CompilerParams(vmem_limit_bytes=LEFT_VMEM_LIMIT),
        cost_estimate=pl.CostEstimate(flops=2 * 2 * HALF * 256 * 256, bytes_accessed=2 * HALF * COLS * 6, transcendentals=0),
        name="left",
    )(half, grad, error, warm_t)


def add_half(combined_ref, factor_ref, acc_ref, gram_ref, tail_ref):
    @pl.loop(0, HALF, step=RIGHT_BLOCK)
    def _(start):
        rows = pl.ds(pl.multiple_of(start, RIGHT_BLOCK), RIGHT_BLOCK)
        factor = factor_ref[rows, :]
        high = factor.astype(jnp.bfloat16)
        middle, low = split2(factor - high.astype(jnp.float32))
        pair = jnp.concatenate([high, middle], axis=1)
        top_high, top_low = split2(combined_ref[0, rows, :])
        bottom_high, bottom_low = split2(combined_ref[1, rows, :])
        acc_ref[...] += mm_t(pair, jnp.concatenate([top_high, bottom_high], axis=1)) + mm_t(pair, jnp.concatenate([top_low, bottom_low], axis=1))
        gram_ref[...] += mm_t(pair, pair)
        tail_ref[...] += mm_t(high, low)


def right_own_kernel(combined_ref, factor_ref, acc_ref, gram_ref, tail_ref):
    for ref in (acc_ref, gram_ref, tail_ref):
        ref[...] = jnp.zeros_like(ref)
    add_half(combined_ref, factor_ref, acc_ref, gram_ref, tail_ref)


def right_other_kernel(combined_ref, factor_ref, acc_in, gram_in, tail_in, right_ref, gram_ref, acc_ref, gram_acc_ref, tail_acc_ref):
    for ref, given in ((acc_ref, acc_in), (gram_acc_ref, gram_in), (tail_acc_ref, tail_in)):
        ref[...] = given[...]
    add_half(combined_ref, factor_ref, acc_ref, gram_acc_ref, tail_acc_ref)
    right = acc_ref[0:128, :] + acc_ref[128:256, :]
    right_ref[...] = right[0:64, 0:128] + right[64:128, 128:256]
    cross = gram_acc_ref[0:128, 128:256] + tail_acc_ref[...]
    gram = gram_acc_ref[0:128, 0:128] + gram_acc_ref[128:256, 128:256] + (cross + cross.T)
    gram_ref[...] = gram[0:64, 0:64] + gram[64:128, 64:128]


def right_own(combined, factor):
    square = jax.ShapeDtypeStruct((256, 256), jnp.float32)
    return pl.pallas_call(
        right_own_kernel,
        out_shape=(square, square, jax.ShapeDtypeStruct((128, 128), jnp.float32)),
        in_specs=[VMEM] * 2,
        out_specs=(VMEM,) * 3,
        compiler_params=pltpu.CompilerParams(vmem_limit_bytes=VMEM_LIMIT),
        cost_estimate=pl.CostEstimate(flops=7 * HALF * 256 * 256, bytes_accessed=ROWS * COLS * 3, transcendentals=0),
        name="right_own",
    )(combined, factor)


def right_other(combined, factor, sums):
    return pl.pallas_call(
        right_other_kernel,
        out_shape=(jax.ShapeDtypeStruct((RANK, COLS), jnp.float32), jax.ShapeDtypeStruct((RANK, RANK), jnp.float32)),
        in_specs=[VMEM] * 5,
        out_specs=(VMEM, VMEM),
        scratch_shapes=[pltpu.VMEM((256, 256), jnp.float32)] * 2 + [pltpu.VMEM((128, 128), jnp.float32)],
        compiler_params=pltpu.CompilerParams(vmem_limit_bytes=VMEM_LIMIT),
        cost_estimate=pl.CostEstimate(flops=7 * HALF * 256 * 256, bytes_accessed=ROWS * COLS * 3, transcendentals=0),
        name="right_other",
    )(combined, factor, *sums)


def inverse_kernel(gram_ref, inverse_ref):
    a = jnp.concatenate([gram_ref[...], jnp.eye(RANK, dtype=jnp.float32)], axis=1)
    for panel in range(0, RANK, 8):
        spread = [jnp.broadcast_to(a[:, panel + k : panel + k + 1], a.shape) for k in range(8)]
        row_at = lax.broadcasted_iota(jnp.int32, a.shape, 0)
        for k in range(8):
            pivot = spread[k][k : k + 1, :]
            row = a[k : k + 1, :]
            inverse_ref[panel + k : panel + k + 1, :] = (row * lax.rsqrt(pivot))[:, RANK:]
            ratio = jnp.where(row_at > k, spread[k] * (1.0 / pivot), 0.0)
            a = a - ratio * row
            for later in range(k + 1, 8):
                spread[later] = spread[later] - ratio * spread[later][k : k + 1, :]
        a = a[8:]


def inverse_lower(gram):
    return pl.pallas_call(
        inverse_kernel,
        out_shape=jax.ShapeDtypeStruct((RANK, RANK), jnp.float32),
        compiler_params=pltpu.CompilerParams(vmem_limit_bytes=VMEM_LIMIT),
        cost_estimate=pl.CostEstimate(flops=RANK**3, bytes_accessed=RANK * RANK * 8, transcendentals=RANK),
        name="inverse",
    )(gram)


def final_kernel(half_ref, own_combined_ref, other_combined_ref, own_ref, other_ref, right_ref, inverse_ref, update_ref, residual_ref, new_q_ref, update_buf, residual_buf, update_sems, residual_sems):
    new_q_t = mm_highest(inverse_ref[...], right_ref[...]) * (1.0 / REPLICAS)
    new_q_ref[...] = new_q_t
    mixed = mm_highest(inverse_ref[...], new_q_t, ((0,), (0,)))
    spread = []
    for part in split2(mixed):
        none = jnp.zeros_like(part)
        two = jnp.concatenate([jnp.concatenate([part, none], axis=1), jnp.concatenate([none, part], axis=1)], axis=0)
        spread.append(jnp.concatenate([two, two], axis=0))
    copies = []
    for h, (combined_ref, factor_ref) in enumerate(((own_combined_ref, own_ref), (other_combined_ref, other_ref))):
        side = half_ref[0] if h == 0 else 1 - half_ref[0]
        start = pl.multiple_of(side * HALF, HALF)
        for k in range(STEPS):
            rows, held, n = pl.ds(k * BLOCK, BLOCK), pl.ds(h * HALF + k * BLOCK, BLOCK), h * STEPS + k
            target = pl.ds(start + k * BLOCK, BLOCK)
            pair = jnp.concatenate(split2(factor_ref[rows, :]), axis=1)
            wide = mm(pair, spread[0]) + mm(pair, spread[1])
            for part in range(2):
                lowrank = wide[:, part * 128 : part * 128 + 128]
                update_buf[part, held, :] = lowrank.astype(jnp.bfloat16)
                residual_buf[part, held, :] = combined_ref[part, rows, :] - lowrank
            for copy in (
                pltpu.make_async_copy(update_buf.at[:, held, :], update_ref.at[:, target, :], update_sems.at[n]),
                pltpu.make_async_copy(residual_buf.at[:, held, :], residual_ref.at[:, target, :], residual_sems.at[n]),
            ):
                copy.start()
                copies.append(copy)
    for copy in copies:
        copy.wait()


def final(half, own_combined, other_combined, own, other, right, inverse):
    return pl.pallas_call(
        final_kernel,
        out_shape=(
            jax.ShapeDtypeStruct((2, ROWS // 2, COLS), jnp.bfloat16),
            jax.ShapeDtypeStruct((2, ROWS // 2, COLS), jnp.float32),
            jax.ShapeDtypeStruct((RANK, COLS), jnp.float32),
        ),
        in_specs=[SMEM] + [VMEM] * 6,
        out_specs=(HBM, HBM, VMEM),
        scratch_shapes=[
            pltpu.VMEM((2, ROWS // 2, COLS), jnp.bfloat16),
            pltpu.VMEM((2, ROWS // 2, COLS), jnp.float32),
            pltpu.SemaphoreType.DMA((2 * STEPS,)),
            pltpu.SemaphoreType.DMA((2 * STEPS,)),
        ],
        compiler_params=pltpu.CompilerParams(vmem_limit_bytes=VMEM_LIMIT),
        cost_estimate=pl.CostEstimate(flops=2 * 2 * HALF * 256 * 256 * 2, bytes_accessed=ROWS * COLS * 6, transcendentals=0),
        name="final",
    )(half, own_combined, other_combined, own, other, right, inverse)


def swap(a):
    return lax.ppermute(a, "c", [(0, 1), (1, 0)])


def scatter_sum(a, axes, count):
    return lax.all_to_all(a, axes, 0, 0, tiled=True).reshape(count, -1, 128).sum(0)


def gather(a, axes, count):
    return lax.all_to_all(jnp.tile(a, (count, 1)), axes, 0, 0, tiled=True)


def sum_over_replicas(a, gram):
    a = a + swap(a)
    for axis in ("y", "x"):
        near, far, back = [lax.ppermute(a, axis, [(i, (i + k) % 4) for i in range(4)]) for k in (1, 2, 3)]
        a = (a + near) + (far + back)
        if axis == "y":
            a, inverse = lax.optimization_barrier((a, inverse_lower(gram)))
    return a, inverse


def combined_half(grad, error, half):
    start = half[0] * HALF
    part = (2, HALF, COLS)
    return lax.dynamic_slice(grad, (0, start, 0), part).astype(jnp.float32) + lax.dynamic_slice(error, (0, start, 0), part)


RING_A = [(i, i ^ 1) for i in range(8)]
RING_B = [(i, (i + 1) % 8 if i % 2 else (i - 1) % 8) for i in range(8)]


def shards(grad, error, warm_q):
    grad = grad.reshape(2, ROWS // 2, COLS)
    error = error.reshape(2, ROWS // 2, COLS)
    warm_t = warm_q.T
    half = lax.axis_index("c").astype(jnp.int32).reshape(1)
    away = left_half(1 - half, grad, error, warm_t)
    keep = left_half(half, grad, error, warm_t)
    piece = scatter_sum(keep + swap(away), ("x", "y"), 16)
    pair = piece + lax.ppermute(piece, "z", RING_A)
    pair, grad, error = lax.optimization_barrier((pair, grad, error))
    near = lax.ppermute(pair, "z", RING_B)
    near, own_combined, grad, error = lax.optimization_barrier((near, combined_half(grad, error, half), grad, error))
    far = lax.ppermute(near, "z", RING_A)
    far, other_combined = lax.optimization_barrier((far, combined_half(grad, error, 1 - half)))
    opposite = lax.ppermute(far, "z", RING_B)
    piece = (pair + near) + (far + opposite)
    own = gather(piece, ("x", "y"), 16)
    other = swap(own)
    sums = right_own(own_combined, own)
    right, gram = right_other(other_combined, other, sums)
    right, inverse = sum_over_replicas(right, gram)
    update, residual, new_q_t = final(half, own_combined, other_combined, own, other, right, inverse)
    return update.reshape(ROWS, COLS), residual.reshape(1, ROWS, COLS), new_q_t.T


def solution(mesh):
    grid = Mesh(mesh.devices.reshape(4, 4, 2, 8), ("x", "y", "c", "z"))
    replicas = ("x", "y", "c")
    return jax.shard_map(
        shards,
        mesh=grid,
        in_specs=(P(replicas, None, "z"), P(replicas, None, "z"), P("z", None)),
        out_specs=(P(None, "z"), P(replicas, None, "z"), P("z", None)),
        check_vma=False,
    )
```

```python
import jax
import jax.numpy as jnp
from jax import lax
from jax.experimental import pallas as pl
from jax.experimental.pallas import tpu as pltpu
from jax.sharding import Mesh, PartitionSpec as P

ROWS = 8192
COLS = 128
RANK = 64
HALF = ROWS // 4
BLOCK = 512
STEPS = HALF // BLOCK
REPLICAS = 32
LEFT_BLOCK = 1024
LEFT_STEPS = HALF // LEFT_BLOCK
RIGHT_BLOCK = 512
VMEM_LIMIT = 24 * 1024 * 1024
LEFT_VMEM_LIMIT = 51 * 1024 * 1024


def split2(a):
    high = a.astype(jnp.bfloat16)
    low = (a - high.astype(jnp.float32)).astype(jnp.bfloat16)
    return high, low


def mm(a, b):
    return jnp.dot(a, b, preferred_element_type=jnp.float32)


def mm_t(a, b):
    return lax.dot_general(a, b, (((0,), (0,)), ((), ())), preferred_element_type=jnp.float32)


def mm_highest(a, b, dims=((1,), (0,))):
    return lax.dot_general(a, b, (dims, ((), ())), precision=lax.Precision.HIGHEST, preferred_element_type=jnp.float32)


def left_kernel(half_ref, grad_ref, error_ref, warm_ref, term_ref, warm_buf, grad_buf, error_buf, warm_sem, grad_sems, error_sems):
    start = pl.multiple_of(half_ref[0] * HALF, HALF)
    warm_copy = pltpu.make_async_copy(warm_ref, warm_buf, warm_sem)
    warm_copy.start()
    copies = []
    for k in range(LEFT_STEPS):
        source, rows = pl.ds(start + k * LEFT_BLOCK, LEFT_BLOCK), pl.ds(k * LEFT_BLOCK, LEFT_BLOCK)
        pair = (
            pltpu.make_async_copy(grad_ref.at[:, source, :], grad_buf.at[:, rows, :], grad_sems.at[k]),
            pltpu.make_async_copy(error_ref.at[:, source, :], error_buf.at[:, rows, :], error_sems.at[k]),
        )
        for copy in pair:
            copy.start()
        copies.append(pair)
    warm_copy.wait()
    high, low = split2(warm_buf[...].T)
    none = jnp.zeros_like(high)
    top_right = jnp.concatenate([high, none, low, none], axis=1)
    bottom_right = jnp.concatenate([none, high, none, low], axis=1)
    top_right = jnp.concatenate([top_right, top_right], axis=0)
    bottom_right = jnp.concatenate([bottom_right, bottom_right], axis=0)
    for k in range(LEFT_STEPS):
        for copy in copies[k]:
            copy.wait()
        rows = pl.ds(k * LEFT_BLOCK, LEFT_BLOCK)
        combined = grad_buf[:, rows, :].astype(jnp.float32) + error_buf[:, rows, :]
        top = jnp.concatenate(split2(combined[0]), axis=1)
        bottom = jnp.concatenate(split2(combined[1]), axis=1)
        wide = mm(top, top_right) + mm(bottom, bottom_right)
        term_ref[rows, :] = wide[:, :128] + wide[:, 128:]


SMEM = pl.BlockSpec(memory_space=pltpu.SMEM)
HBM = pl.BlockSpec(memory_space=pltpu.HBM)
VMEM = pl.BlockSpec(memory_space=pltpu.VMEM)


def left_half(half, grad, error, warm_t):
    return pl.pallas_call(
        left_kernel,
        out_shape=jax.ShapeDtypeStruct((HALF, 128), jnp.float32),
        in_specs=[SMEM, HBM, HBM, HBM],
        out_specs=VMEM,
        scratch_shapes=[
            pltpu.VMEM((RANK, COLS), jnp.float32),
            pltpu.VMEM((2, HALF, COLS), jnp.bfloat16),
            pltpu.VMEM((2, HALF, COLS), jnp.float32),
            pltpu.SemaphoreType.DMA,
            pltpu.SemaphoreType.DMA((LEFT_STEPS,)),
            pltpu.SemaphoreType.DMA((LEFT_STEPS,)),
        ],
        compiler_params=pltpu.CompilerParams(vmem_limit_bytes=LEFT_VMEM_LIMIT),
        cost_estimate=pl.CostEstimate(flops=2 * 2 * HALF * 256 * 256, bytes_accessed=2 * HALF * COLS * 6, transcendentals=0),
        name="left",
    )(half, grad, error, warm_t)


def add_half(combined_ref, factor_ref, acc_ref, gram_ref, tail_ref):
    @pl.loop(0, HALF, step=RIGHT_BLOCK)
    def _(start):
        rows = pl.ds(pl.multiple_of(start, RIGHT_BLOCK), RIGHT_BLOCK)
        factor = factor_ref[rows, :]
        high = factor.astype(jnp.bfloat16)
        middle, low = split2(factor - high.astype(jnp.float32))
        pair = jnp.concatenate([high, middle], axis=1)
        top_high, top_low = split2(combined_ref[0, rows, :])
        bottom_high, bottom_low = split2(combined_ref[1, rows, :])
        acc_ref[...] += mm_t(pair, jnp.concatenate([top_high, bottom_high], axis=1)) + mm_t(pair, jnp.concatenate([top_low, bottom_low], axis=1))
        gram_ref[...] += mm_t(pair, pair)
        tail_ref[...] += mm_t(high, low)


def right_own_kernel(combined_ref, factor_ref, acc_ref, gram_ref, tail_ref):
    for ref in (acc_ref, gram_ref, tail_ref):
        ref[...] = jnp.zeros_like(ref)
    add_half(combined_ref, factor_ref, acc_ref, gram_ref, tail_ref)


def right_other_kernel(combined_ref, factor_ref, acc_in, gram_in, tail_in, right_ref, gram_ref, acc_ref, gram_acc_ref, tail_acc_ref):
    for ref, given in ((acc_ref, acc_in), (gram_acc_ref, gram_in), (tail_acc_ref, tail_in)):
        ref[...] = given[...]
    add_half(combined_ref, factor_ref, acc_ref, gram_acc_ref, tail_acc_ref)
    right = acc_ref[0:128, :] + acc_ref[128:256, :]
    right_ref[...] = right[0:64, 0:128] + right[64:128, 128:256]
    cross = gram_acc_ref[0:128, 128:256] + tail_acc_ref[...]
    gram = gram_acc_ref[0:128, 0:128] + gram_acc_ref[128:256, 128:256] + (cross + cross.T)
    gram_ref[...] = gram[0:64, 0:64] + gram[64:128, 64:128]


def right_own(combined, factor):
    square = jax.ShapeDtypeStruct((256, 256), jnp.float32)
    return pl.pallas_call(
        right_own_kernel,
        out_shape=(square, square, jax.ShapeDtypeStruct((128, 128), jnp.float32)),
        in_specs=[VMEM] * 2,
        out_specs=(VMEM,) * 3,
        compiler_params=pltpu.CompilerParams(vmem_limit_bytes=VMEM_LIMIT),
        cost_estimate=pl.CostEstimate(flops=7 * HALF * 256 * 256, bytes_accessed=ROWS * COLS * 3, transcendentals=0),
        name="right_own",
    )(combined, factor)


def right_other(combined, factor, sums):
    return pl.pallas_call(
        right_other_kernel,
        out_shape=(jax.ShapeDtypeStruct((RANK, COLS), jnp.float32), jax.ShapeDtypeStruct((RANK, RANK), jnp.float32)),
        in_specs=[VMEM] * 5,
        out_specs=(VMEM, VMEM),
        scratch_shapes=[pltpu.VMEM((256, 256), jnp.float32)] * 2 + [pltpu.VMEM((128, 128), jnp.float32)],
        compiler_params=pltpu.CompilerParams(vmem_limit_bytes=VMEM_LIMIT),
        cost_estimate=pl.CostEstimate(flops=7 * HALF * 256 * 256, bytes_accessed=ROWS * COLS * 3, transcendentals=0),
        name="right_other",
    )(combined, factor, *sums)


def inverse_kernel(gram_ref, inverse_ref):
    a = jnp.concatenate([gram_ref[...], jnp.eye(RANK, dtype=jnp.float32)], axis=1)
    for panel in range(0, RANK, 8):
        spread = [jnp.broadcast_to(a[:, panel + k : panel + k + 1], a.shape) for k in range(8)]
        row_at = lax.broadcasted_iota(jnp.int32, a.shape, 0)
        for k in range(8):
            pivot = spread[k][k : k + 1, :]
            row = a[k : k + 1, :]
            inverse_ref[panel + k : panel + k + 1, :] = (row * lax.rsqrt(pivot))[:, RANK:]
            ratio = jnp.where(row_at > k, spread[k] * (1.0 / pivot), 0.0)
            a = a - ratio * row
            for later in range(k + 1, 8):
                spread[later] = spread[later] - ratio * spread[later][k : k + 1, :]
        a = a[8:]


def inverse_lower(gram):
    return pl.pallas_call(
        inverse_kernel,
        out_shape=jax.ShapeDtypeStruct((RANK, RANK), jnp.float32),
        compiler_params=pltpu.CompilerParams(vmem_limit_bytes=VMEM_LIMIT),
        cost_estimate=pl.CostEstimate(flops=RANK**3, bytes_accessed=RANK * RANK * 8, transcendentals=RANK),
        name="inverse",
    )(gram)


def final_kernel(half_ref, own_combined_ref, other_combined_ref, own_ref, other_ref, right_ref, inverse_ref, update_ref, residual_ref, new_q_ref, update_buf, residual_buf, update_sems, residual_sems):
    new_q_t = mm_highest(inverse_ref[...], right_ref[...]) * (1.0 / REPLICAS)
    new_q_ref[...] = new_q_t
    mixed = mm_highest(inverse_ref[...], new_q_t, ((0,), (0,)))
    spread = []
    for part in split2(mixed):
        none = jnp.zeros_like(part)
        two = jnp.concatenate([jnp.concatenate([part, none], axis=1), jnp.concatenate([none, part], axis=1)], axis=0)
        spread.append(jnp.concatenate([two, two], axis=0))
    copies = []
    for h, (combined_ref, factor_ref) in enumerate(((own_combined_ref, own_ref), (other_combined_ref, other_ref))):
        side = half_ref[0] if h == 0 else 1 - half_ref[0]
        start = pl.multiple_of(side * HALF, HALF)
        for k in range(STEPS):
            rows, held, n = pl.ds(k * BLOCK, BLOCK), pl.ds(h * HALF + k * BLOCK, BLOCK), h * STEPS + k
            target = pl.ds(start + k * BLOCK, BLOCK)
            pair = jnp.concatenate(split2(factor_ref[rows, :]), axis=1)
            wide = mm(pair, spread[0]) + mm(pair, spread[1])
            for part in range(2):
                lowrank = wide[:, part * 128 : part * 128 + 128]
                update_buf[part, held, :] = lowrank.astype(jnp.bfloat16)
                residual_buf[part, held, :] = combined_ref[part, rows, :] - lowrank
            for copy in (
                pltpu.make_async_copy(update_buf.at[:, held, :], update_ref.at[:, target, :], update_sems.at[n]),
                pltpu.make_async_copy(residual_buf.at[:, held, :], residual_ref.at[:, target, :], residual_sems.at[n]),
            ):
                copy.start()
                copies.append(copy)
    for copy in copies:
        copy.wait()


def final(half, own_combined, other_combined, own, other, right, inverse):
    return pl.pallas_call(
        final_kernel,
        out_shape=(
            jax.ShapeDtypeStruct((2, ROWS // 2, COLS), jnp.bfloat16),
            jax.ShapeDtypeStruct((2, ROWS // 2, COLS), jnp.float32),
            jax.ShapeDtypeStruct((RANK, COLS), jnp.float32),
        ),
        in_specs=[SMEM] + [VMEM] * 6,
        out_specs=(HBM, HBM, VMEM),
        scratch_shapes=[
            pltpu.VMEM((2, ROWS // 2, COLS), jnp.bfloat16),
            pltpu.VMEM((2, ROWS // 2, COLS), jnp.float32),
            pltpu.SemaphoreType.DMA((2 * STEPS,)),
            pltpu.SemaphoreType.DMA((2 * STEPS,)),
        ],
        compiler_params=pltpu.CompilerParams(vmem_limit_bytes=VMEM_LIMIT),
        cost_estimate=pl.CostEstimate(flops=2 * 2 * HALF * 256 * 256 * 2, bytes_accessed=ROWS * COLS * 6, transcendentals=0),
        name="final",
    )(half, own_combined, other_combined, own, other, right, inverse)


def swap(a):
    return lax.ppermute(a, "c", [(0, 1), (1, 0)])


def scatter_sum(a, axes, count):
    return lax.all_to_all(a, axes, 0, 0, tiled=True).reshape(count, -1, 128).sum(0)


def gather(a, axes, count):
    return lax.all_to_all(jnp.tile(a, (count, 1)), axes, 0, 0, tiled=True)


def sum_of_four(a, axis):
    places = range(0, lax.axis_size(axis), 4)
    others = [lax.ppermute(a, axis, [(p + i, p + (i ^ k)) for p in places for i in range(4)]) for k in (1, 2, 3)]
    return (a + others[0]) + (others[1] + others[2])


def sum_over_replicas(a, gram):
    a = sum_of_four(a + swap(a), "y")
    a, inverse = lax.optimization_barrier((a, inverse_lower(gram)))
    return sum_of_four(a, "x"), inverse


def combined_half(grad, error, half):
    start = half[0] * HALF
    part = (2, HALF, COLS)
    return lax.dynamic_slice(grad, (0, start, 0), part).astype(jnp.float32) + lax.dynamic_slice(error, (0, start, 0), part)


def shards(grad, error, warm_q):
    grad = grad.reshape(2, ROWS // 2, COLS)
    error = error.reshape(2, ROWS // 2, COLS)
    warm_t = warm_q.T
    half = lax.axis_index("c").astype(jnp.int32).reshape(1)
    away = left_half(1 - half, grad, error, warm_t)
    keep = left_half(half, grad, error, warm_t)
    piece = scatter_sum(keep + swap(away), ("x", "y"), 16)
    piece, grad, error = lax.optimization_barrier((sum_of_four(piece, "z"), grad, error))
    piece = piece + lax.ppermute(piece, "z", [(i, 7 - i) for i in range(8)])
    own_combined = combined_half(grad, error, half)
    own_combined, grad, error = lax.optimization_barrier((own_combined, grad, error))
    other_combined = combined_half(grad, error, 1 - half)
    piece, own_combined, other_combined = lax.optimization_barrier((piece, own_combined, other_combined))
    own = gather(piece, ("x", "y"), 16)
    other = swap(own)
    sums = right_own(own_combined, own)
    right, gram = right_other(other_combined, other, sums)
    right, inverse = sum_over_replicas(right, gram)
    update, residual, new_q_t = final(half, own_combined, other_combined, own, other, right, inverse)
    return update.reshape(ROWS, COLS), residual.reshape(1, ROWS, COLS), new_q_t.T


def solution(mesh):
    grid = Mesh(mesh.devices.reshape(4, 4, 2, 8), ("x", "y", "c", "z"))
    replicas = ("x", "y", "c")
    return jax.shard_map(
        shards,
        mesh=grid,
        in_specs=(P(replicas, None, "z"), P(replicas, None, "z"), P("z", None)),
        out_specs=(P(None, "z"), P(replicas, None, "z"), P("z", None)),
        check_vma=False,
    )
```

```python
import jax
import jax.numpy as jnp
from jax import lax
from jax.experimental import pallas as pl
from jax.experimental.pallas import tpu as pltpu
from jax.sharding import Mesh, PartitionSpec as P

ROWS = 8192
COLS = 128
RANK = 64
HALF = ROWS // 4
BLOCK = 512
STEPS = HALF // BLOCK
REPLICAS = 32
LEFT_BLOCK = 1024
LEFT_STEPS = HALF // LEFT_BLOCK
RIGHT_BLOCK = 1024
VMEM_LIMIT = 24 * 1024 * 1024
LEFT_VMEM_LIMIT = 51 * 1024 * 1024


def split2(a):
    high = a.astype(jnp.bfloat16)
    low = (a - high.astype(jnp.float32)).astype(jnp.bfloat16)
    return high, low


def mm(a, b):
    return jnp.dot(a, b, preferred_element_type=jnp.float32)


def mm_t(a, b):
    return lax.dot_general(a, b, (((0,), (0,)), ((), ())), preferred_element_type=jnp.float32)


def mm_highest(a, b, dims=((1,), (0,))):
    return lax.dot_general(a, b, (dims, ((), ())), precision=lax.Precision.HIGHEST, preferred_element_type=jnp.float32)


def left_kernel(half_ref, grad_ref, error_ref, warm_ref, term_ref, warm_buf, grad_buf, error_buf, warm_sem, grad_sems, error_sems):
    start = pl.multiple_of(half_ref[0] * HALF, HALF)
    warm_copy = pltpu.make_async_copy(warm_ref, warm_buf, warm_sem)
    warm_copy.start()
    copies = []
    for k in range(LEFT_STEPS):
        source, rows = pl.ds(start + k * LEFT_BLOCK, LEFT_BLOCK), pl.ds(k * LEFT_BLOCK, LEFT_BLOCK)
        pair = (
            pltpu.make_async_copy(grad_ref.at[:, source, :], grad_buf.at[:, rows, :], grad_sems.at[k]),
            pltpu.make_async_copy(error_ref.at[:, source, :], error_buf.at[:, rows, :], error_sems.at[k]),
        )
        for copy in pair:
            copy.start()
        copies.append(pair)
    warm_copy.wait()
    high, low = split2(warm_buf[...].T)
    none = jnp.zeros_like(high)
    top_right = jnp.concatenate([high, none, low, none], axis=1)
    bottom_right = jnp.concatenate([none, high, none, low], axis=1)
    top_right = jnp.concatenate([top_right, top_right], axis=0)
    bottom_right = jnp.concatenate([bottom_right, bottom_right], axis=0)
    for k in range(LEFT_STEPS):
        for copy in copies[k]:
            copy.wait()
        rows = pl.ds(k * LEFT_BLOCK, LEFT_BLOCK)
        combined = grad_buf[:, rows, :].astype(jnp.float32) + error_buf[:, rows, :]
        top = jnp.concatenate(split2(combined[0]), axis=1)
        bottom = jnp.concatenate(split2(combined[1]), axis=1)
        wide = mm(top, top_right) + mm(bottom, bottom_right)
        term_ref[rows, :] = wide[:, :128] + wide[:, 128:]


SMEM = pl.BlockSpec(memory_space=pltpu.SMEM)
HBM = pl.BlockSpec(memory_space=pltpu.HBM)
VMEM = pl.BlockSpec(memory_space=pltpu.VMEM)


def left_half(half, grad, error, warm_t):
    return pl.pallas_call(
        left_kernel,
        out_shape=jax.ShapeDtypeStruct((HALF, 128), jnp.float32),
        in_specs=[SMEM, HBM, HBM, HBM],
        out_specs=VMEM,
        scratch_shapes=[
            pltpu.VMEM((RANK, COLS), jnp.float32),
            pltpu.VMEM((2, HALF, COLS), jnp.bfloat16),
            pltpu.VMEM((2, HALF, COLS), jnp.float32),
            pltpu.SemaphoreType.DMA,
            pltpu.SemaphoreType.DMA((LEFT_STEPS,)),
            pltpu.SemaphoreType.DMA((LEFT_STEPS,)),
        ],
        compiler_params=pltpu.CompilerParams(vmem_limit_bytes=LEFT_VMEM_LIMIT),
        cost_estimate=pl.CostEstimate(flops=2 * 2 * HALF * 256 * 256, bytes_accessed=2 * HALF * COLS * 6, transcendentals=0),
        name="left",
    )(half, grad, error, warm_t)


def add_half(combined_ref, factor_ref, acc_ref, gram_ref, tail_ref):
    @pl.loop(0, HALF, step=RIGHT_BLOCK)
    def _(start):
        rows = pl.ds(pl.multiple_of(start, RIGHT_BLOCK), RIGHT_BLOCK)
        factor = factor_ref[rows, :]
        high = factor.astype(jnp.bfloat16)
        middle, low = split2(factor - high.astype(jnp.float32))
        pair = jnp.concatenate([high, middle], axis=1)
        top_high, top_low = split2(combined_ref[0, rows, :])
        bottom_high, bottom_low = split2(combined_ref[1, rows, :])
        acc_ref[...] += mm_t(pair, jnp.concatenate([top_high, bottom_high], axis=1)) + mm_t(pair, jnp.concatenate([top_low, bottom_low], axis=1))
        gram_ref[...] += mm_t(pair, pair)
        tail_ref[...] += mm_t(high, low)


def right_own_kernel(combined_ref, factor_ref, acc_ref, gram_ref, tail_ref):
    for ref in (acc_ref, gram_ref, tail_ref):
        ref[...] = jnp.zeros_like(ref)
    add_half(combined_ref, factor_ref, acc_ref, gram_ref, tail_ref)


def right_other_kernel(combined_ref, factor_ref, acc_in, gram_in, tail_in, right_ref, gram_ref, acc_ref, gram_acc_ref, tail_acc_ref):
    for ref, given in ((acc_ref, acc_in), (gram_acc_ref, gram_in), (tail_acc_ref, tail_in)):
        ref[...] = given[...]
    add_half(combined_ref, factor_ref, acc_ref, gram_acc_ref, tail_acc_ref)
    right = acc_ref[0:128, :] + acc_ref[128:256, :]
    right_ref[...] = right[0:64, 0:128] + right[64:128, 128:256]
    cross = gram_acc_ref[0:128, 128:256] + tail_acc_ref[...]
    gram = gram_acc_ref[0:128, 0:128] + gram_acc_ref[128:256, 128:256] + (cross + cross.T)
    gram_ref[...] = gram[0:64, 0:64] + gram[64:128, 64:128]


def right_own(combined, factor):
    square = jax.ShapeDtypeStruct((256, 256), jnp.float32)
    return pl.pallas_call(
        right_own_kernel,
        out_shape=(square, square, jax.ShapeDtypeStruct((128, 128), jnp.float32)),
        in_specs=[VMEM] * 2,
        out_specs=(VMEM,) * 3,
        compiler_params=pltpu.CompilerParams(vmem_limit_bytes=VMEM_LIMIT),
        cost_estimate=pl.CostEstimate(flops=7 * HALF * 256 * 256, bytes_accessed=ROWS * COLS * 3, transcendentals=0),
        name="right_own",
    )(combined, factor)


def right_other(combined, factor, sums):
    return pl.pallas_call(
        right_other_kernel,
        out_shape=(jax.ShapeDtypeStruct((RANK, COLS), jnp.float32), jax.ShapeDtypeStruct((RANK, RANK), jnp.float32)),
        in_specs=[VMEM] * 5,
        out_specs=(VMEM, VMEM),
        scratch_shapes=[pltpu.VMEM((256, 256), jnp.float32)] * 2 + [pltpu.VMEM((128, 128), jnp.float32)],
        compiler_params=pltpu.CompilerParams(vmem_limit_bytes=VMEM_LIMIT),
        cost_estimate=pl.CostEstimate(flops=7 * HALF * 256 * 256, bytes_accessed=ROWS * COLS * 3, transcendentals=0),
        name="right_other",
    )(combined, factor, *sums)


def inverse_kernel(gram_ref, inverse_ref):
    a = jnp.concatenate([gram_ref[...], jnp.eye(RANK, dtype=jnp.float32)], axis=1)
    for panel in range(0, RANK, 8):
        spread = [jnp.broadcast_to(a[:, panel + k : panel + k + 1], a.shape) for k in range(8)]
        row_at = lax.broadcasted_iota(jnp.int32, a.shape, 0)
        for k in range(8):
            pivot = spread[k][k : k + 1, :]
            row = a[k : k + 1, :]
            inverse_ref[panel + k : panel + k + 1, :] = (row * lax.rsqrt(pivot))[:, RANK:]
            ratio = jnp.where(row_at > k, spread[k] * (1.0 / pivot), 0.0)
            a = a - ratio * row
            for later in range(k + 1, 8):
                spread[later] = spread[later] - ratio * spread[later][k : k + 1, :]
        a = a[8:]


def inverse_lower(gram):
    return pl.pallas_call(
        inverse_kernel,
        out_shape=jax.ShapeDtypeStruct((RANK, RANK), jnp.float32),
        compiler_params=pltpu.CompilerParams(vmem_limit_bytes=VMEM_LIMIT),
        cost_estimate=pl.CostEstimate(flops=RANK**3, bytes_accessed=RANK * RANK * 8, transcendentals=RANK),
        name="inverse",
    )(gram)


def final_kernel(half_ref, own_combined_ref, other_combined_ref, own_ref, other_ref, right_ref, inverse_ref, update_ref, residual_ref, new_q_ref, update_buf, residual_buf, update_sems, residual_sems):
    new_q_t = mm_highest(inverse_ref[...], right_ref[...]) * (1.0 / REPLICAS)
    new_q_ref[...] = new_q_t
    mixed = mm_highest(inverse_ref[...], new_q_t, ((0,), (0,)))
    spread = []
    for part in split2(mixed):
        none = jnp.zeros_like(part)
        two = jnp.concatenate([jnp.concatenate([part, none], axis=1), jnp.concatenate([none, part], axis=1)], axis=0)
        spread.append(jnp.concatenate([two, two], axis=0))
    copies = []
    for h, (combined_ref, factor_ref) in enumerate(((own_combined_ref, own_ref), (other_combined_ref, other_ref))):
        side = half_ref[0] if h == 0 else 1 - half_ref[0]
        start = pl.multiple_of(side * HALF, HALF)
        for k in range(STEPS):
            rows, held, n = pl.ds(k * BLOCK, BLOCK), pl.ds(h * HALF + k * BLOCK, BLOCK), h * STEPS + k
            target = pl.ds(start + k * BLOCK, BLOCK)
            pair = jnp.concatenate(split2(factor_ref[rows, :]), axis=1)
            wide = mm(pair, spread[0]) + mm(pair, spread[1])
            for part in range(2):
                lowrank = wide[:, part * 128 : part * 128 + 128]
                update_buf[part, held, :] = lowrank.astype(jnp.bfloat16)
                residual_buf[part, held, :] = combined_ref[part, rows, :] - lowrank
            for copy in (
                pltpu.make_async_copy(update_buf.at[:, held, :], update_ref.at[:, target, :], update_sems.at[n]),
                pltpu.make_async_copy(residual_buf.at[:, held, :], residual_ref.at[:, target, :], residual_sems.at[n]),
            ):
                copy.start()
                copies.append(copy)
    for copy in copies:
        copy.wait()


def final(half, own_combined, other_combined, own, other, right, inverse):
    return pl.pallas_call(
        final_kernel,
        out_shape=(
            jax.ShapeDtypeStruct((2, ROWS // 2, COLS), jnp.bfloat16),
            jax.ShapeDtypeStruct((2, ROWS // 2, COLS), jnp.float32),
            jax.ShapeDtypeStruct((RANK, COLS), jnp.float32),
        ),
        in_specs=[SMEM] + [VMEM] * 6,
        out_specs=(HBM, HBM, VMEM),
        scratch_shapes=[
            pltpu.VMEM((2, ROWS // 2, COLS), jnp.bfloat16),
            pltpu.VMEM((2, ROWS // 2, COLS), jnp.float32),
            pltpu.SemaphoreType.DMA((2 * STEPS,)),
            pltpu.SemaphoreType.DMA((2 * STEPS,)),
        ],
        compiler_params=pltpu.CompilerParams(vmem_limit_bytes=VMEM_LIMIT),
        cost_estimate=pl.CostEstimate(flops=2 * 2 * HALF * 256 * 256 * 2, bytes_accessed=ROWS * COLS * 6, transcendentals=0),
        name="final",
    )(half, own_combined, other_combined, own, other, right, inverse)


def swap(a):
    return lax.ppermute(a, "c", [(0, 1), (1, 0)])


def scatter_sum(a, axes, count):
    return lax.all_to_all(a, axes, 0, 0, tiled=True).reshape(count, -1, 128).sum(0)


def gather(a, axes, count):
    return lax.all_to_all(jnp.tile(a, (count, 1)), axes, 0, 0, tiled=True)


def sum_of_four(a, axis):
    places = range(0, lax.axis_size(axis), 4)
    others = [lax.ppermute(a, axis, [(p + i, p + (i ^ k)) for p in places for i in range(4)]) for k in (1, 2, 3)]
    return (a + others[0]) + (others[1] + others[2])


def sum_over_replicas(a, gram):
    a = sum_of_four(a + swap(a), "y")
    a, inverse = lax.optimization_barrier((a, inverse_lower(gram)))
    return sum_of_four(a, "x"), inverse


def combined_half(grad, error, half):
    start = half[0] * HALF
    part = (2, HALF, COLS)
    return lax.dynamic_slice(grad, (0, start, 0), part).astype(jnp.float32) + lax.dynamic_slice(error, (0, start, 0), part)


def shards(grad, error, warm_q):
    grad = grad.reshape(2, ROWS // 2, COLS)
    error = error.reshape(2, ROWS // 2, COLS)
    warm_t = warm_q.T
    half = lax.axis_index("c").astype(jnp.int32).reshape(1)
    away = left_half(1 - half, grad, error, warm_t)
    keep = left_half(half, grad, error, warm_t)
    piece = scatter_sum(keep + swap(away), ("x", "y"), 16)
    piece, grad, error = lax.optimization_barrier((sum_of_four(piece, "z"), grad, error))
    piece = piece + lax.ppermute(piece, "z", [(i, 7 - i) for i in range(8)])
    own_combined = combined_half(grad, error, half)
    own_combined, grad, error = lax.optimization_barrier((own_combined, grad, error))
    other_combined = combined_half(grad, error, 1 - half)
    piece, own_combined, other_combined = lax.optimization_barrier((piece, own_combined, other_combined))
    own = gather(piece, ("x", "y"), 16)
    other = swap(own)
    sums = right_own(own_combined, own)
    right, gram = right_other(other_combined, other, sums)
    right, inverse = sum_over_replicas(right, gram)
    update, residual, new_q_t = final(half, own_combined, other_combined, own, other, right, inverse)
    return update.reshape(ROWS, COLS), residual.reshape(1, ROWS, COLS), new_q_t.T


def solution(mesh):
    grid = Mesh(mesh.devices.reshape(4, 4, 2, 8), ("x", "y", "c", "z"))
    replicas = ("x", "y", "c")
    return jax.shard_map(
        shards,
        mesh=grid,
        in_specs=(P(replicas, None, "z"), P(replicas, None, "z"), P("z", None)),
        out_specs=(P(None, "z"), P(replicas, None, "z"), P("z", None)),
        check_vma=False,
    )
```
